128 devices in a mesh: doc: 16 (over y, z), own: 8 (over x, core).
Axes of the slice: x: 4, y: 4, z: 4, core: 2. Of those that a mesh axis runs over, the one named last changes fastest.
Arguments:
- embeddings: bfloat16 [65536, 768], P(('doc', 'own')), may hold values from -6 to 6
- cluster_ids: int32 [65536], P(('doc', 'own')), may hold values from 0 to 50175, as said below
- keep_flags: int32 [65536], P(('doc', 'own')), may hold values 0 or 1
Outputs:
- centroids: bfloat16 [50176, 768], P(('doc', 'own'))
- scores: float32 [65536], P(('doc', 'own'))
The draws below stay inside these ranges and needn't reach their ends.
Inputs may be any that keep to these rules, and one draw needn't show every extreme that they name: `cluster_ids`: cluster c is held by device c // 392 of the rows' order. Among the rows of one device, at most 8 name clusters held by any one device, and exactly 8 do for one device.
All inputs are finite; a program needn't handle non-finite values. No bound on the sum of `keep_flags` on one device may be relied on, other than what follows from the above.
Results may differ from the reference program's by a relative error of at most 0.0015.
Values may be sent and summed in bfloat16 or wider, within the bound.
No kernel may reach another device: no remote copies, remote signals or barrier semaphores. Data moves between devices by JAX's collectives and lax.ppermute only.
A program may use at most 64 MiB of HBM per device.

```python
import math
import jax
import jax.numpy as jnp
from jax import lax

D = 768
CLUSTER_DEV = 392
ROW_DEV = 512
GRID = 128
CLUSTERS = 50176
ROWS = 65536
CAPF = 8


def draw_cluster_ids(key, part):
    keys = jax.random.split(key, 5)
    position = jnp.arange(ROW_DEV, dtype=jnp.int32)[None, :]
    busy = jax.random.randint(keys[0], (GRID, 1), 0, GRID)
    offset = jax.random.randint(keys[1], (GRID, 1), 0, GRID - 1)
    spread = (busy + 1 + (position - CAPF + offset) % (GRID - 1)) % GRID
    target = jnp.where(position < CAPF, busy, spread)
    block_keys = jax.random.split(keys[2], GRID)
    target = jax.vmap(jax.random.permutation)(block_keys, target)
    first = jax.random.randint(keys[3], (GRID, ROW_DEV), 0, CLUSTER_DEV)
    second = jax.random.randint(keys[4], (GRID, ROW_DEV), 0, CLUSTER_DEV)
    local_id = first * second // CLUSTER_DEV
    return (target * CLUSTER_DEV + local_id).reshape(-1).astype(jnp.int32)


def set_ends(array, key, low, high):
    spot = [jax.random.randint(jax.random.fold_in(key, axis), (), 0, length) for axis, length in enumerate(array.shape)]
    main_axis = array.shape.index(max(array.shape))
    beside = spot[:main_axis] + [(spot[main_axis] + 1) % array.shape[main_axis]] + spot[main_axis + 1:]
    return array.at[tuple(spot)].set(low).at[tuple(beside)].set(high)


def block_levels(stream_key, shape, pieces, low, top_value):
    level = 1.0
    for axis_at, parts in pieces:
        heights = jax.random.uniform(jax.random.fold_in(jax.random.fold_in(stream_key, 6), axis_at), (parts,), jnp.float32, low / len(pieces), top_value / len(pieces))
        level = level * jnp.repeat(jnp.exp(heights), shape[axis_at] // parts).reshape((-1,) + (1,) * (len(shape) - 1 - axis_at))
    return level


def scatter_about(rng, shape, scale, bound, pieces=(), kind=jnp.bfloat16):
    values = scale * jax.random.normal(rng, shape, jnp.float32)
    if pieces:
        values = values * block_levels(rng, shape, pieces, -0.22, 0.18)
    return jnp.clip(values, -bound, bound).astype(kind)


def setup_inputs(seed: int = 0) -> dict:
    key_list = jax.random.split(jax.random.key(seed), 4)
    embeddings = scatter_about(key_list[0], (ROWS, D), 1.0, 6.0, ((0, 128),))
    cluster_ids = draw_cluster_ids(jax.random.fold_in(key_list[3], 71), 0)
    keep_flags = set_ends((jax.random.randint(key_list[2], (ROWS,), 0, 4) < 3).astype(jnp.int32), jax.random.fold_in(key_list[2], 1), 0, 1)
    return {"embeddings": embeddings, "cluster_ids": cluster_ids, "keep_flags": keep_flags}


def reference(embeddings, cluster_ids, keep_flags):
    weighted = embeddings.astype(jnp.float32) * keep_flags.astype(jnp.float32)[:, None]
    kept_sum = jax.ops.segment_sum(weighted, cluster_ids, num_segments=CLUSTERS)
    inv_scale = lax.rsqrt(lax.optimization_barrier(jnp.mean(kept_sum * kept_sum, axis=1, keepdims=True)) + 1e-06) / math.sqrt(D)
    centroids = (kept_sum * inv_scale).astype(jnp.bfloat16)
    picked = jnp.take(centroids, cluster_ids.astype(jnp.int32), axis=0)
    as_float = embeddings.astype(jnp.float32)
    products = lax.optimization_barrier(jnp.sum(as_float * picked.astype(jnp.float32), axis=1))
    row_scale = lax.rsqrt(lax.optimization_barrier(jnp.mean(as_float * as_float, axis=1)) + 1e-06) / math.sqrt(D)
    return (centroids, products * row_scale)
```

```python
import math

import jax
import jax.numpy as jnp
from jax import lax
from jax.sharding import PartitionSpec as P

CLUSTER_DEV = 392
AXES = ("doc", "own")
CODE_BASE = 16
CODE_LANES = 128


def body(embeddings, cluster_ids, keep_flags):
    row_count, width = embeddings.shape
    grid_size = lax.axis_size(AXES)
    capacity = 2 * row_count // grid_size
    slots_total = grid_size * capacity
    target = cluster_ids // CLUSTER_DEV
    local_id = cluster_ids % CLUSTER_DEV
    hits = (target[:, None] == jnp.arange(grid_size, dtype=jnp.int32)[None, :]).astype(jnp.bfloat16)
    rows = jnp.arange(row_count, dtype=jnp.int32)
    earlier = (rows[:, None] > rows[None, :]).astype(jnp.bfloat16)
    before = jnp.dot(earlier, hits, preferred_element_type=jnp.float32)
    position = jnp.sum(before * hits.astype(jnp.float32), axis=1).astype(jnp.int32)
    slot = target * capacity + position
    place = (jnp.arange(slots_total, dtype=jnp.int32)[:, None] == slot[None, :]).astype(jnp.bfloat16)
    lane = jnp.arange(CODE_LANES, dtype=jnp.int32)[None, :]
    codes = jnp.where(lane == 0, local_id[:, None] // CODE_BASE + 1, 0)
    codes = jnp.where(lane == 1, local_id[:, None] % CODE_BASE, codes)
    codes = jnp.where(lane == 2, keep_flags[:, None], codes)
    wide = jnp.concatenate([embeddings, codes.astype(jnp.bfloat16)], axis=1)
    outgoing = jnp.dot(place, wide, preferred_element_type=jnp.float32).astype(jnp.bfloat16)
    arrived = lax.all_to_all(outgoing, AXES, split_axis=0, concat_axis=0, tiled=True)
    row_scale = lax.rsqrt(
        jnp.mean(jnp.square(embeddings.astype(jnp.float32)), axis=1) + 1e-06
    ) / math.sqrt(width)
    code = arrived[:, width:width + 3].astype(jnp.int32)
    arrived = arrived[:, :width]
    owner = code[:, 0] * CODE_BASE + code[:, 1] - CODE_BASE
    labels = jnp.arange(CLUSTER_DEV, dtype=jnp.int32)
    match = labels[:, None] == owner[None, :]
    table = jnp.where(match, code[:, 2][None, :], 0).astype(jnp.bfloat16)
    sums = jnp.dot(table, arrived, preferred_element_type=jnp.float32)
    inv_scale = lax.rsqrt(jnp.mean(sums * sums, axis=1, keepdims=True) + 1e-06) / math.sqrt(width)
    centroids = (sums * inv_scale).astype(jnp.bfloat16)
    similar = lax.dot_general(
        centroids, arrived, (((1,), (1,)), ((), ())), preferred_element_type=jnp.float32
    )
    products = jnp.sum(jnp.where(match, similar, 0.0), axis=0)
    returned = lax.all_to_all(products, AXES, split_axis=0, concat_axis=0, tiled=True)
    scores = returned[slot] * row_scale
    return (centroids, scores)


def solution(mesh):
    in_specs = (P(AXES, None), P(AXES), P(AXES))
    out_specs = (P(AXES, None), P(AXES))
    return jax.shard_map(body, mesh=mesh, in_specs=in_specs, out_specs=out_specs, check_vma=False)
```

```python
import math

import jax
import jax.numpy as jnp
from jax import lax
from jax.experimental import pallas as pl
from jax.experimental.pallas import tpu as pltpu
from jax.sharding import PartitionSpec as P

AXES = ("doc", "own")
CLUSTER_DEV = 392
CLUSTER_PAD = 400
DEVICES = 128
CAP = 8
SLOTS = DEVICES * CAP
ROWS = 512
WIDTH = 768
LANES = 128
WIDE = WIDTH + LANES
CODE_BASE = 16
PARTS = 4
PART = SLOTS // PARTS
PACK_VMEM = 63 * 1024 * 1024
VMEM_LIMIT = 48 * 1024 * 1024

NN = (((1,), (0,)), ((), ()))
NT = (((1,), (1,)), ((), ()))


def iota(shape, axis):
    return lax.broadcasted_iota(jnp.int32, shape, axis)


def matmul(a, b, dims=NN):
    return lax.dot_general(a, b, dims, preferred_element_type=jnp.float32)


def as_bf16(mask):
    return jnp.where(mask, 1.0, 0.0).astype(jnp.bfloat16)


def split3(x):
    high = x.astype(jnp.bfloat16)
    rest = x - high.astype(jnp.float32)
    middle = rest.astype(jnp.bfloat16)
    low = (rest - middle.astype(jnp.float32)).astype(jnp.bfloat16)
    return high, middle, low


def owner_device(ids):
    return ((ids >> 3) * 5350) >> 18


def pack_kernel(ids_ref, keep_ref, emb_hbm, out_hbm, slot_ref, emb, staged, in_sem, out_sem):
    load = pltpu.make_async_copy(emb_hbm, emb, in_sem)
    load.start()
    ids = ids_ref[...]
    target = owner_device(ids)
    local = ids - target * CLUSTER_DEV
    hits = iota((DEVICES, ROWS), 0) == target
    ones_bf = as_bf16(hits)
    earlier = as_bf16(iota((LANES, LANES), 0) < iota((LANES, LANES), 1))
    every = jnp.ones((LANES, LANES), jnp.bfloat16)
    before, offset = [], None
    for k in range(ROWS // LANES):
        block = ones_bf[:, k * LANES:(k + 1) * LANES]
        count = matmul(block, earlier)
        before.append(count if offset is None else count + offset)
        total = matmul(block, every)
        offset = total if offset is None else offset + total
    counts = jnp.concatenate(before, axis=1)
    position = jnp.sum(jnp.where(hits, counts, 0.0), axis=0, keepdims=True)
    slot = target * CAP + position.astype(jnp.int32)
    slot_ref[...] = slot
    row = iota((LANES, ROWS), 0)
    codes = jnp.where(row == 0, (local >> 4) + 1, 0)
    codes = jnp.where(row == 1, local & (CODE_BASE - 1), codes)
    codes = jnp.where(row == 2, keep_ref[...], codes)
    codes = codes.astype(jnp.float32).astype(jnp.bfloat16)
    load.wait()
    copies = []
    for k in range(PARTS):
        here = pl.ds(k * PART, PART)
        place = as_bf16(iota((PART, ROWS), 0) + k * PART == slot)
        staged[here, :WIDTH] = matmul(place, emb[...]).astype(jnp.bfloat16)
        staged[here, WIDTH:] = matmul(place, codes, NT).astype(jnp.bfloat16)
        copy = pltpu.make_async_copy(staged.at[here], out_hbm.at[here], out_sem.at[k])
        copy.start()
        copies.append(copy)
    for copy in copies:
        copy.wait()


def pack(embeddings, ids, keep):
    vmem = pl.BlockSpec(memory_space=pltpu.VMEM)
    hbm = pl.BlockSpec(memory_space=pltpu.HBM)
    return pl.pallas_call(
        pack_kernel,
        out_shape=(
            jax.ShapeDtypeStruct((SLOTS, WIDE), jnp.bfloat16),
            jax.ShapeDtypeStruct((1, ROWS), jnp.int32),
        ),
        in_specs=[vmem, vmem, hbm],
        out_specs=(hbm, vmem),
        scratch_shapes=[
            pltpu.VMEM((ROWS, WIDTH), jnp.bfloat16),
            pltpu.VMEM((SLOTS, WIDE), jnp.bfloat16),
            pltpu.SemaphoreType.DMA,
            pltpu.SemaphoreType.DMA((PARTS,)),
        ],
        compiler_params=pltpu.CompilerParams(vmem_limit_bytes=PACK_VMEM),
    )(ids, keep, embeddings)


def middle_kernel(arrived, centroids_hbm, products_ref, centroids, out_sem):
    pick = as_bf16(
        (iota((CAP, LANES), 0) == iota((CAP, LANES), 1))
    )
    codes = matmul(pick, arrived[:, WIDTH:], NT)
    owner = codes[0:1].astype(jnp.int32) * CODE_BASE + codes[1:2].astype(jnp.int32) - CODE_BASE
    keep = codes[2:3] > 0.5
    match = iota((CLUSTER_PAD, SLOTS), 0) == owner
    rows = arrived[:, :WIDTH]
    sums = matmul(as_bf16(match & keep), rows)
    inv_scale = lax.rsqrt(
        jnp.sum(sums * sums, axis=1, keepdims=True) * (1.0 / WIDTH) + 1e-06
    ) / math.sqrt(WIDTH)
    unit = (sums * inv_scale).astype(jnp.bfloat16)
    centroids[...] = unit[:CLUSTER_DEV]
    store = pltpu.make_async_copy(centroids, centroids_hbm, out_sem)
    store.start()
    similar = matmul(unit, rows, NT)
    products = jnp.sum(jnp.where(match, similar, 0.0), axis=0, keepdims=True)
    mine = iota((DEVICES, SLOTS), 1) // CAP == iota((DEVICES, SLOTS), 0)
    spread = as_bf16(iota((SLOTS, LANES), 0) % CAP == iota((SLOTS, LANES), 1))
    total = None
    for part in split3(products):
        term = matmul(jnp.where(mine, part.astype(jnp.float32), 0.0).astype(jnp.bfloat16), spread)
        total = term if total is None else total + term
    products_ref[...] = total
    store.wait()


def middle(arrived):
    vmem = pl.BlockSpec(memory_space=pltpu.VMEM)
    hbm = pl.BlockSpec(memory_space=pltpu.HBM)
    return pl.pallas_call(
        middle_kernel,
        out_shape=(
            jax.ShapeDtypeStruct((CLUSTER_DEV, WIDTH), jnp.bfloat16),
            jax.ShapeDtypeStruct((DEVICES, LANES), jnp.float32),
        ),
        in_specs=[vmem],
        out_specs=(hbm, vmem),
        scratch_shapes=[
            pltpu.VMEM((CLUSTER_DEV, WIDTH), jnp.bfloat16),
            pltpu.SemaphoreType.DMA,
        ],
        compiler_params=pltpu.CompilerParams(vmem_limit_bytes=VMEM_LIMIT),
    )(arrived)


def final_kernel(returned_ref, slot_ref, scale_ref, scores_ref):
    slot = slot_ref[...]
    hits = as_bf16(iota((DEVICES, ROWS), 0) == slot // CAP)
    back = returned_ref[...].T[:CAP]
    total = None
    for part in split3(back):
        term = matmul(part, hits)
        total = term if total is None else total + term
    chosen = jnp.where(iota((CAP, ROWS), 0) == slot % CAP, total, 0.0)
    scores_ref[...] = jnp.sum(chosen, axis=0, keepdims=True) * scale_ref[...]


def final(returned, slot, scale):
    vmem = pl.BlockSpec(memory_space=pltpu.VMEM)
    return pl.pallas_call(
        final_kernel,
        out_shape=jax.ShapeDtypeStruct((1, ROWS), jnp.float32),
        in_specs=[vmem] * 3,
        out_specs=vmem,
        compiler_params=pltpu.CompilerParams(vmem_limit_bytes=16 * 1024 * 1024),
    )(returned, slot, scale)


def body(embeddings, cluster_ids, keep_flags):
    outgoing, slot = pack(embeddings, cluster_ids.reshape(1, ROWS), keep_flags.reshape(1, ROWS))
    arrived = lax.all_to_all(outgoing, AXES, split_axis=0, concat_axis=0, tiled=True)
    row_scale = lax.rsqrt(
        jnp.mean(jnp.square(embeddings.astype(jnp.float32)), axis=1) + 1e-06
    ) / math.sqrt(WIDTH)
    centroids, products = middle(arrived)
    returned = lax.all_to_all(products, AXES, split_axis=0, concat_axis=0, tiled=True)
    scores = final(returned, slot, row_scale.reshape(1, ROWS))
    return (centroids, scores.reshape(ROWS))


def solution(mesh):
    in_specs = (P(AXES, None), P(AXES), P(AXES))
    out_specs = (P(AXES, None), P(AXES))
    return jax.shard_map(body, mesh=mesh, in_specs=in_specs, out_specs=out_specs, check_vma=False)
```

```python
import math

import jax
import jax.numpy as jnp
from jax import lax
from jax.experimental import pallas as pl
from jax.experimental.pallas import tpu as pltpu
from jax.sharding import PartitionSpec as P

AXES = ("doc", "own")
CLUSTER_DEV = 392
CLUSTER_PAD = 400
DEVICES = 128
CAP = 8
SLOTS = DEVICES * CAP
ROWS = 512
WIDTH = 768
LANES = 128
SUB = 4
PER = CAP // SUB
DATA_TILES = WIDTH // LANES * PER
GROUP = LANES // CAP
CODE_BASE = 16
CODE_KEEP = 32
PARTS = 4
PART = SLOTS // PARTS
PART_PEERS = DEVICES // PARTS
PACK_VMEM = 63 * 1024 * 1024
VMEM_LIMIT = 48 * 1024 * 1024

NN = (((1,), (0,)), ((), ()))
NT = (((1,), (1,)), ((), ()))


def iota(shape, axis):
    return lax.broadcasted_iota(jnp.int32, shape, axis)


def matmul(a, b, dims=NN):
    return lax.dot_general(a, b, dims, preferred_element_type=jnp.float32)


def as_bf16(mask):
    return jnp.where(mask, 1.0, 0.0).astype(jnp.bfloat16)


def split3(x):
    high = x.astype(jnp.bfloat16)
    rest = x - high.astype(jnp.float32)
    middle = rest.astype(jnp.bfloat16)
    low = (rest - middle.astype(jnp.float32)).astype(jnp.bfloat16)
    return high, middle, low


def owner_device(ids):
    return ((ids >> 3) * 5350) >> 18


def pack_kernel(
    ids_hbm, keep_hbm, emb_hbm, out_hbm, slot_hbm, ids_ref, keep_ref, emb, staged, codes, slots, in_sem, out_sem
):
    loads = [
        pltpu.make_async_copy(source, kept, in_sem.at[k])
        for k, (source, kept) in enumerate(((ids_hbm, ids_ref), (keep_hbm, keep_ref), (emb_hbm, emb)))
    ]
    for load in loads:
        load.start()
    loads[0].wait()
    loads[1].wait()
    ids = ids_ref[...]
    target = owner_device(ids)
    local = ids - target * CLUSTER_DEV
    hits = iota((DEVICES, ROWS), 0) == target
    hits_bf = as_bf16(hits)
    earlier = as_bf16(iota((LANES, LANES), 0) < iota((LANES, LANES), 1))
    every = jnp.ones((LANES, LANES), jnp.bfloat16)
    before, offset = [], None
    blocks = ROWS // LANES
    for k in range(blocks):
        block = hits_bf[:, k * LANES:(k + 1) * LANES]
        count = matmul(block, earlier)
        before.append(count if offset is None else count + offset)
        if k < blocks - 1:
            total = matmul(block, every)
            offset = total if offset is None else offset + total
    counts = jnp.concatenate(before, axis=1)
    position = jnp.sum(jnp.where(hits, counts, 0.0), axis=0, keepdims=True).astype(jnp.int32)
    slot = target * CAP + position
    slots[...] = slot
    stores = [pltpu.make_async_copy(slots, slot_hbm, out_sem.at[0])]
    stores[-1].start()
    at_slot = iota((LANES, ROWS), 0) & (CAP - 1) == position
    upper = (local >> 4) + 1 + CODE_KEEP * keep_ref[...]
    lower = local & (CODE_BASE - 1)
    coded = [
        matmul(hits_bf, jnp.where(at_slot, part, 0).astype(jnp.float32).astype(jnp.bfloat16), NT)
        for part in (upper, lower)
    ]
    which = iota((DEVICES, SUB, LANES), 1)
    tile = jnp.where(which == 1, coded[1][:, None, :], 0.0)
    tile = jnp.where(which == 0, coded[0][:, None, :], tile)
    codes[...] = tile.astype(jnp.bfloat16)
    stores.append(pltpu.make_async_copy(codes, out_hbm.at[:, DATA_TILES], out_sem.at[1]))
    stores[-1].start()
    loads[2].wait()
    for k in range(PARTS):
        place = as_bf16(iota((PART, ROWS), 0) + k * PART == slot)
        block = matmul(place, emb[...]).astype(jnp.bfloat16)
        peers = pl.ds(k * PART_PEERS, PART_PEERS)
        for c in range(WIDTH // LANES):
            piece = block[:, c * LANES:(c + 1) * LANES].reshape(PART_PEERS, PER, SUB, LANES)
            staged[peers, c * PER:(c + 1) * PER] = piece
        stores.append(
            pltpu.make_async_copy(staged.at[peers], out_hbm.at[peers, pl.ds(0, DATA_TILES)], out_sem.at[2 + k])
        )
        stores[-1].start()
    for store in stores:
        store.wait()


def pack(ids, keep, embeddings):
    hbm = pl.BlockSpec(memory_space=pl.ANY)
    return pl.pallas_call(
        pack_kernel,
        out_shape=(
            jax.ShapeDtypeStruct((DEVICES, DATA_TILES + 1, SUB, LANES), jnp.bfloat16),
            jax.ShapeDtypeStruct((1, ROWS), jnp.int32),
        ),
        in_specs=[hbm] * 3,
        out_specs=(hbm, hbm),
        scratch_shapes=[
            pltpu.VMEM((1, ROWS), jnp.int32),
            pltpu.VMEM((1, ROWS), jnp.int32),
            pltpu.VMEM((ROWS, WIDTH), jnp.bfloat16),
            pltpu.VMEM((DEVICES, DATA_TILES, SUB, LANES), jnp.bfloat16),
            pltpu.VMEM((DEVICES, SUB, LANES), jnp.bfloat16),
            pltpu.VMEM((1, ROWS), jnp.int32),
            pltpu.SemaphoreType.DMA((3,)),
            pltpu.SemaphoreType.DMA((2 + PARTS,)),
        ],
        compiler_params=pltpu.CompilerParams(vmem_limit_bytes=PACK_VMEM),
    )(ids, keep, embeddings)


def middle_kernel(arrived, centroids_hbm, products_hbm, centroids, products_ref, out_sem):
    flat = (DEVICES * SUB, LANES)
    codes = arrived[:, DATA_TILES].reshape(flat)
    place = (iota(flat, 0) >> 2) & (GROUP - 1) == iota(flat, 1) >> 3
    codes = jnp.where(place, codes.astype(jnp.float32), 0.0).astype(jnp.bfloat16)
    row, column = iota((CAP, DEVICES * SUB), 0), iota((CAP, DEVICES * SUB), 1)
    part = column & (SUB - 1)
    weight = jnp.where(part == 0, CODE_BASE, jnp.where(part == 1, 1, 0))
    weight = jnp.where(column >> 6 == row, weight, 0)
    code = matmul(weight.astype(jnp.float32).astype(jnp.bfloat16), codes).astype(jnp.int32)
    code = jnp.concatenate([code[k:k + 1] for k in range(CAP)], axis=1)
    keep_base = CODE_BASE * CODE_KEEP
    owner = (code & (keep_base - 1)) - CODE_BASE
    kept = jnp.where(code >= keep_base, owner, -1)
    rows = jnp.concatenate(
        [arrived[:, c * PER:(c + 1) * PER].reshape(SLOTS, LANES) for c in range(WIDTH // LANES)], axis=1
    )
    labels = iota((CLUSTER_PAD, SLOTS), 0)
    sums = matmul(as_bf16(labels == kept), rows)
    inv_scale = lax.rsqrt(
        jnp.sum(sums * sums, axis=1, keepdims=True) * (1.0 / WIDTH) + 1e-06
    ) / math.sqrt(WIDTH)
    unit = (sums * inv_scale).astype(jnp.bfloat16)
    centroids[...] = unit[:CLUSTER_DEV]
    stores = [pltpu.make_async_copy(centroids, centroids_hbm, out_sem.at[0])]
    stores[-1].start()
    similar = matmul(unit, rows, NT)
    products = jnp.sum(jnp.where(labels == owner, similar, 0.0), axis=0, keepdims=True)
    spread = jnp.concatenate(
        [jnp.broadcast_to(products[:, k * LANES:(k + 1) * LANES], (GROUP, LANES)) for k in range(CAP)], axis=0
    )
    square = (DEVICES, LANES)
    products_ref[...] = jnp.where(iota(square, 0) & (GROUP - 1) == iota(square, 1) >> 3, spread, 0.0)
    stores.append(pltpu.make_async_copy(products_ref, products_hbm, out_sem.at[1]))
    stores[-1].start()
    for store in stores:
        store.wait()


def middle(arrived):
    vmem = pl.BlockSpec(memory_space=pltpu.VMEM)
    hbm = pl.BlockSpec(memory_space=pl.ANY)
    return pl.pallas_call(
        middle_kernel,
        out_shape=(
            jax.ShapeDtypeStruct((CLUSTER_DEV, WIDTH), jnp.bfloat16),
            jax.ShapeDtypeStruct((DEVICES, LANES), jnp.float32),
        ),
        in_specs=[vmem],
        out_specs=(hbm, hbm),
        scratch_shapes=[
            pltpu.VMEM((CLUSTER_DEV, WIDTH), jnp.bfloat16),
            pltpu.VMEM((DEVICES, LANES), jnp.float32),
            pltpu.SemaphoreType.DMA((2,)),
        ],
        compiler_params=pltpu.CompilerParams(vmem_limit_bytes=VMEM_LIMIT),
    )(arrived)


def final_kernel(returned_ref, slot_ref, scale_ref, scores_ref):
    slot = slot_ref[...]
    hits = as_bf16(iota((DEVICES, ROWS), 0) == slot >> 3)
    back = jnp.sum(returned_ref[...].T.reshape(GROUP, CAP, DEVICES), axis=0)
    total = None
    for part in split3(back):
        term = matmul(part, hits)
        total = term if total is None else total + term
    chosen = jnp.where(iota((CAP, ROWS), 0) == slot & (CAP - 1), total, 0.0)
    scores_ref[...] = jnp.sum(chosen, axis=0, keepdims=True) * scale_ref[...]


def final(returned, slot, scale):
    vmem = pl.BlockSpec(memory_space=pltpu.VMEM)
    return pl.pallas_call(
        final_kernel,
        out_shape=jax.ShapeDtypeStruct((1, ROWS), jnp.float32),
        in_specs=[vmem] * 3,
        out_specs=vmem,
        compiler_params=pltpu.CompilerParams(vmem_limit_bytes=16 * 1024 * 1024),
    )(returned, slot, scale)


def body(embeddings, cluster_ids, keep_flags):
    outgoing, slot = pack(cluster_ids.reshape(1, ROWS), keep_flags.reshape(1, ROWS), embeddings)
    arrived = lax.all_to_all(outgoing, AXES, split_axis=0, concat_axis=0, tiled=True)
    row_scale = lax.rsqrt(
        jnp.mean(jnp.square(embeddings.astype(jnp.float32)), axis=1) + 1e-06
    ) / math.sqrt(WIDTH)
    centroids, products = middle(arrived)
    returned = lax.all_to_all(products, AXES, split_axis=0, concat_axis=0, tiled=True)
    scores = final(returned, slot, row_scale.reshape(1, ROWS))
    return (centroids, scores.reshape(ROWS))


def solution(mesh):
    in_specs = (P(AXES, None), P(AXES), P(AXES))
    out_specs = (P(AXES, None), P(AXES))
    return jax.shard_map(body, mesh=mesh, in_specs=in_specs, out_specs=out_specs, check_vma=False)
```

```python
import math

import jax
import jax.numpy as jnp
from jax import lax
from jax.experimental import pallas as pl
from jax.experimental.pallas import tpu as pltpu
from jax.sharding import PartitionSpec as P

AXES = ("doc", "own")
CLUSTER_DEV = 392
CHUNKS = ((0, 208, 208), (208, 192, 184))
DEVICES = 128
CAP = 8
SLOTS = DEVICES * CAP
ROWS = 512
WIDTH = 768
LANES = 128
SUB = 4
PER = CAP // SUB
DATA_TILES = WIDTH // LANES * PER
GROUP = LANES // CAP
CODE_BASE = 16
CODE_KEEP = 32
PARTS = (256, 256, 256, 128, 128)
PACK_VMEM = 63 * 1024 * 1024
VMEM_LIMIT = 48 * 1024 * 1024

NN = (((1,), (0,)), ((), ()))
NT = (((1,), (1,)), ((), ()))


def iota(shape, axis):
    return lax.broadcasted_iota(jnp.int32, shape, axis)


def matmul(a, b, dims=NN):
    return lax.dot_general(a, b, dims, preferred_element_type=jnp.float32)


def as_bf16(mask):
    return jnp.where(mask, 1.0, 0.0).astype(jnp.bfloat16)


def split3(x):
    high = x.astype(jnp.bfloat16)
    rest = x - high.astype(jnp.float32)
    middle = rest.astype(jnp.bfloat16)
    low = (rest - middle.astype(jnp.float32)).astype(jnp.bfloat16)
    return high, middle, low


def owner_device(ids):
    return ((ids >> 3) * 5350) >> 18


def pack_kernel(
    ids_hbm, keep_hbm, emb_hbm, out_hbm, slot_hbm, ids_ref, keep_ref, emb, staged, codes, slots, in_sem, out_sem
):
    loads = [
        pltpu.make_async_copy(source, kept, in_sem.at[k])
        for k, (source, kept) in enumerate(((ids_hbm, ids_ref), (keep_hbm, keep_ref), (emb_hbm, emb)))
    ]
    for load in loads:
        load.start()
    loads[0].wait()
    loads[1].wait()
    ids = ids_ref[...]
    target = owner_device(ids)
    local = ids - target * CLUSTER_DEV
    hits = iota((DEVICES, ROWS), 0) == target
    hits_bf = as_bf16(hits)
    earlier = as_bf16(iota((LANES, LANES), 0) < iota((LANES, LANES), 1))
    every = jnp.ones((LANES, LANES), jnp.bfloat16)
    before, offset = [], None
    blocks = ROWS // LANES
    for k in range(blocks):
        block = hits_bf[:, k * LANES:(k + 1) * LANES]
        count = matmul(block, earlier)
        before.append(count if offset is None else count + offset)
        if k < blocks - 1:
            total = matmul(block, every)
            offset = total if offset is None else offset + total
    counts = jnp.concatenate(before, axis=1)
    position = jnp.sum(jnp.where(hits, counts, 0.0), axis=0, keepdims=True).astype(jnp.int32)
    slot = target * CAP + position
    slots[...] = slot
    stores = [pltpu.make_async_copy(slots, slot_hbm, out_sem.at[0])]
    stores[-1].start()
    at_slot = iota((LANES, ROWS), 0) & (CAP - 1) == position
    upper = (local >> 4) + 1 + CODE_KEEP * keep_ref[...]
    lower = local & (CODE_BASE - 1)
    coded = [
        matmul(hits_bf, jnp.where(at_slot, part, 0).astype(jnp.float32).astype(jnp.bfloat16), NT)
        for part in (upper, lower)
    ]
    which = iota((DEVICES, SUB, LANES), 1)
    tile = jnp.where(which == 1, coded[1][:, None, :], 0.0)
    tile = jnp.where(which == 0, coded[0][:, None, :], tile)
    codes[...] = tile.astype(jnp.bfloat16)
    stores.append(pltpu.make_async_copy(codes, out_hbm.at[:, DATA_TILES], out_sem.at[1]))
    stores[-1].start()
    loads[2].wait()
    first = 0
    for k, count in enumerate(PARTS):
        place = as_bf16(iota((count, ROWS), 0) + first == slot)
        block = matmul(place, emb[...]).astype(jnp.bfloat16)
        peers = pl.ds(first // CAP, count // CAP)
        for c in range(WIDTH // LANES):
            piece = block[:, c * LANES:(c + 1) * LANES].reshape(count // CAP, PER, SUB, LANES)
            staged[peers, c * PER:(c + 1) * PER] = piece
        stores.append(
            pltpu.make_async_copy(staged.at[peers], out_hbm.at[peers, pl.ds(0, DATA_TILES)], out_sem.at[2 + k])
        )
        stores[-1].start()
        first += count
    for store in stores:
        store.wait()


def pack(ids, keep, embeddings):
    hbm = pl.BlockSpec(memory_space=pl.ANY)
    return pl.pallas_call(
        pack_kernel,
        out_shape=(
            jax.ShapeDtypeStruct((DEVICES, DATA_TILES + 1, SUB, LANES), jnp.bfloat16),
            jax.ShapeDtypeStruct((1, ROWS), jnp.int32),
        ),
        in_specs=[hbm] * 3,
        out_specs=(hbm, hbm),
        scratch_shapes=[
            pltpu.VMEM((1, ROWS), jnp.int32),
            pltpu.VMEM((1, ROWS), jnp.int32),
            pltpu.VMEM((ROWS, WIDTH), jnp.bfloat16),
            pltpu.VMEM((DEVICES, DATA_TILES, SUB, LANES), jnp.bfloat16),
            pltpu.VMEM((DEVICES, SUB, LANES), jnp.bfloat16),
            pltpu.VMEM((1, ROWS), jnp.int32),
            pltpu.SemaphoreType.DMA((3,)),
            pltpu.SemaphoreType.DMA((2 + len(PARTS),)),
        ],
        compiler_params=pltpu.CompilerParams(vmem_limit_bytes=PACK_VMEM),
    )(ids, keep, embeddings)


def middle_kernel(arrived, centroids_hbm, products_hbm, centroids, products_ref, out_sem):
    flat = (DEVICES * SUB, LANES)
    codes = arrived[:, DATA_TILES].reshape(flat)
    place = (iota(flat, 0) >> 2) & (GROUP - 1) == iota(flat, 1) >> 3
    codes = jnp.where(place, codes.astype(jnp.float32), 0.0).astype(jnp.bfloat16)
    row, column = iota((CAP, DEVICES * SUB), 0), iota((CAP, DEVICES * SUB), 1)
    part = column & (SUB - 1)
    weight = jnp.where(part == 0, CODE_BASE, jnp.where(part == 1, 1, 0))
    weight = jnp.where(column >> 6 == row, weight, 0)
    code = matmul(weight.astype(jnp.float32).astype(jnp.bfloat16), codes).astype(jnp.int32)
    code = jnp.concatenate([code[k:k + 1] for k in range(CAP)], axis=1)
    keep_base = CODE_BASE * CODE_KEEP
    owner = (code & (keep_base - 1)) - CODE_BASE
    kept = jnp.where(code >= keep_base, owner, -1)
    rows = jnp.concatenate(
        [arrived[:, c * PER:(c + 1) * PER].reshape(SLOTS, LANES) for c in range(WIDTH // LANES)], axis=1
    )
    labels = [iota((count, SLOTS), 0) + start for start, count, _ in CHUNKS]
    sums = [matmul(as_bf16(label == kept), rows) for label in labels]
    stores, products = [], None
    for k, (start, _, real) in enumerate(CHUNKS):
        inv_scale = lax.rsqrt(
            jnp.sum(sums[k] * sums[k], axis=1, keepdims=True) * (1.0 / WIDTH) + 1e-06
        ) / math.sqrt(WIDTH)
        unit = (sums[k] * inv_scale).astype(jnp.bfloat16)
        here = pl.ds(start, real)
        centroids[here] = unit[:real]
        stores.append(pltpu.make_async_copy(centroids.at[here], centroids_hbm.at[here], out_sem.at[k]))
        stores[-1].start()
        similar = matmul(unit, rows, NT)
        part = jnp.sum(jnp.where(labels[k] == owner, similar, 0.0), axis=0, keepdims=True)
        products = part if products is None else products + part
    spread = jnp.concatenate(
        [jnp.broadcast_to(products[:, k * LANES:(k + 1) * LANES], (GROUP, LANES)) for k in range(CAP)], axis=0
    )
    square = (DEVICES, LANES)
    products_ref[...] = jnp.where(iota(square, 0) & (GROUP - 1) == iota(square, 1) >> 3, spread, 0.0)
    stores.append(pltpu.make_async_copy(products_ref, products_hbm, out_sem.at[len(CHUNKS)]))
    stores[-1].start()
    for store in stores:
        store.wait()


def middle(arrived):
    vmem = pl.BlockSpec(memory_space=pltpu.VMEM)
    hbm = pl.BlockSpec(memory_space=pl.ANY)
    return pl.pallas_call(
        middle_kernel,
        out_shape=(
            jax.ShapeDtypeStruct((CLUSTER_DEV, WIDTH), jnp.bfloat16),
            jax.ShapeDtypeStruct((DEVICES, LANES), jnp.float32),
        ),
        in_specs=[vmem],
        out_specs=(hbm, hbm),
        scratch_shapes=[
            pltpu.VMEM((CLUSTER_DEV, WIDTH), jnp.bfloat16),
            pltpu.VMEM((DEVICES, LANES), jnp.float32),
            pltpu.SemaphoreType.DMA((len(CHUNKS) + 1,)),
        ],
        compiler_params=pltpu.CompilerParams(vmem_limit_bytes=VMEM_LIMIT),
    )(arrived)


def final_kernel(returned_ref, slot_ref, scale_ref, scores_ref):
    slot = slot_ref[...]
    hits = as_bf16(iota((DEVICES, ROWS), 0) == slot >> 3)
    back = jnp.sum(returned_ref[...].T.reshape(GROUP, CAP, DEVICES), axis=0)
    total = None
    for part in split3(back):
        term = matmul(part, hits)
        total = term if total is None else total + term
    chosen = jnp.where(iota((CAP, ROWS), 0) == slot & (CAP - 1), total, 0.0)
    scores_ref[...] = jnp.sum(chosen, axis=0, keepdims=True) * scale_ref[...]


def final(returned, slot, scale):
    vmem = pl.BlockSpec(memory_space=pltpu.VMEM)
    return pl.pallas_call(
        final_kernel,
        out_shape=jax.ShapeDtypeStruct((1, ROWS), jnp.float32),
        in_specs=[vmem] * 3,
        out_specs=vmem,
        compiler_params=pltpu.CompilerParams(vmem_limit_bytes=16 * 1024 * 1024),
    )(returned, slot, scale)


def body(embeddings, cluster_ids, keep_flags):
    outgoing, slot = pack(cluster_ids.reshape(1, ROWS), keep_flags.reshape(1, ROWS), embeddings)
    arrived = lax.all_to_all(outgoing, AXES, split_axis=0, concat_axis=0, tiled=True)
    row_scale = lax.rsqrt(
        jnp.mean(jnp.square(embeddings.astype(jnp.float32)), axis=1) + 1e-06
    ) / math.sqrt(WIDTH)
    centroids, products = middle(arrived)
    returned = lax.all_to_all(products, AXES, split_axis=0, concat_axis=0, tiled=True)
    scores = final(returned, slot, row_scale.reshape(1, ROWS))
    return (centroids, scores.reshape(ROWS))


def solution(mesh):
    in_specs = (P(AXES, None), P(AXES), P(AXES))
    out_specs = (P(AXES, None), P(AXES))
    return jax.shard_map(body, mesh=mesh, in_specs=in_specs, out_specs=out_specs, check_vma=False)
```

```python
import math

import jax
import jax.numpy as jnp
from jax import lax
from jax.experimental import pallas as pl
from jax.experimental.pallas import tpu as pltpu
from jax.sharding import PartitionSpec as P

AXES = ("doc", "own")
CLUSTER_DEV = 392
CHUNKS = ((0, 208, 208), (208, 192, 184))
DEVICES = 128
CAP = 8
SLOTS = DEVICES * CAP
ROWS = 512
WIDTH = 768
LANES = 128
SUB = 4
PER = CAP // SUB
DATA_TILES = WIDTH // LANES * PER
GROUP = LANES // CAP
CODE_BASE = 16
CODE_KEEP = 32
PARTS = (256, 256, 256, 128, 128)
PACK_VMEM = 63 * 1024 * 1024
VMEM_LIMIT = 48 * 1024 * 1024

NN = (((1,), (0,)), ((), ()))
NT = (((1,), (1,)), ((), ()))


def iota(shape, axis):
    return lax.broadcasted_iota(jnp.int32, shape, axis)


def matmul(a, b, dims=NN):
    return lax.dot_general(a, b, dims, preferred_element_type=jnp.float32)


def as_bf16(mask):
    return jnp.where(mask, 1.0, 0.0).astype(jnp.bfloat16)


def split3(x):
    high = x.astype(jnp.bfloat16)
    rest = x - high.astype(jnp.float32)
    middle = rest.astype(jnp.bfloat16)
    low = (rest - middle.astype(jnp.float32)).astype(jnp.bfloat16)
    return high, middle, low


def owner_device(ids):
    return ((ids >> 3) * 5350) >> 18


def pack_kernel(
    ids_hbm, keep_hbm, emb_hbm, out_hbm, slot_hbm, ids_ref, keep_ref, emb, staged, codes, slots, in_sem, out_sem
):
    loads = [
        pltpu.make_async_copy(source, kept, in_sem.at[k])
        for k, (source, kept) in enumerate(((ids_hbm, ids_ref), (keep_hbm, keep_ref), (emb_hbm, emb)))
    ]
    for load in loads:
        load.start()
    loads[0].wait()
    loads[1].wait()
    ids = ids_ref[...]
    target = owner_device(ids)
    local = ids - target * CLUSTER_DEV
    hits = iota((DEVICES, ROWS), 0) == target
    hits_bf = as_bf16(hits)
    earlier = as_bf16(iota((LANES, LANES), 0) < iota((LANES, LANES), 1))
    every = jnp.ones((LANES, LANES), jnp.bfloat16)
    before, offset = [], None
    blocks = ROWS // LANES
    for k in range(blocks):
        block = hits_bf[:, k * LANES:(k + 1) * LANES]
        count = matmul(block, earlier)
        before.append(count if offset is None else count + offset)
        if k < blocks - 1:
            total = matmul(block, every)
            offset = total if offset is None else offset + total
    counts = jnp.concatenate(before, axis=1)
    position = jnp.sum(jnp.where(hits, counts, 0.0), axis=0, keepdims=True).astype(jnp.int32)
    slot = target * CAP + position
    slots[...] = slot
    stores = [pltpu.make_async_copy(slots, slot_hbm, out_sem.at[0])]
    stores[-1].start()
    at_slot = iota((LANES, ROWS), 0) & (CAP - 1) == position
    upper = (local >> 4) + 1 + CODE_KEEP * keep_ref[...]
    lower = local & (CODE_BASE - 1)
    coded = [
        matmul(hits_bf, jnp.where(at_slot, part, 0).astype(jnp.float32).astype(jnp.bfloat16), NT)
        for part in (upper, lower)
    ]
    which = iota((DEVICES, SUB, LANES), 1)
    tile = jnp.where(which == 1, coded[1][:, None, :], 0.0)
    tile = jnp.where(which == 0, coded[0][:, None, :], tile)
    codes[...] = tile.astype(jnp.bfloat16)
    stores.append(pltpu.make_async_copy(codes, out_hbm.at[:, DATA_TILES], out_sem.at[1]))
    stores[-1].start()
    loads[2].wait()
    first = 0
    for k, count in enumerate(PARTS):
        place = as_bf16(iota((count, ROWS), 0) + first == slot)
        block = matmul(place, emb[...])
        peers = pl.ds(first // CAP, count // CAP)
        for c in range(WIDTH // LANES):
            piece = block[:, c * LANES:(c + 1) * LANES].reshape(count // CAP, PER, SUB, LANES)
            staged[peers, c * PER:(c + 1) * PER] = piece.astype(jnp.bfloat16)
        stores.append(
            pltpu.make_async_copy(staged.at[peers], out_hbm.at[peers, pl.ds(0, DATA_TILES)], out_sem.at[2 + k])
        )
        stores[-1].start()
        first += count
    for store in stores:
        store.wait()


def pack(ids, keep, embeddings):
    hbm = pl.BlockSpec(memory_space=pl.ANY)
    return pl.pallas_call(
        pack_kernel,
        out_shape=(
            jax.ShapeDtypeStruct((DEVICES, DATA_TILES + 1, SUB, LANES), jnp.bfloat16),
            jax.ShapeDtypeStruct((1, ROWS), jnp.int32),
        ),
        in_specs=[hbm] * 3,
        out_specs=(hbm, hbm),
        scratch_shapes=[
            pltpu.VMEM((1, ROWS), jnp.int32),
            pltpu.VMEM((1, ROWS), jnp.int32),
            pltpu.VMEM((ROWS, WIDTH), jnp.bfloat16),
            pltpu.VMEM((DEVICES, DATA_TILES, SUB, LANES), jnp.bfloat16),
            pltpu.VMEM((DEVICES, SUB, LANES), jnp.bfloat16),
            pltpu.VMEM((1, ROWS), jnp.int32),
            pltpu.SemaphoreType.DMA((3,)),
            pltpu.SemaphoreType.DMA((2 + len(PARTS),)),
        ],
        compiler_params=pltpu.CompilerParams(vmem_limit_bytes=PACK_VMEM),
    )(ids, keep, embeddings)


def middle_kernel(
    arrived, emb_hbm, centroids_hbm, products_hbm, scale_ref, emb, centroids, products_ref, in_sem, out_sem
):
    load = pltpu.make_async_copy(emb_hbm, emb, in_sem)
    load.start()
    flat = (DEVICES * SUB, LANES)
    codes = arrived[:, DATA_TILES].reshape(flat)
    place = (iota(flat, 0) >> 2) & (GROUP - 1) == iota(flat, 1) >> 3
    codes = jnp.where(place, codes.astype(jnp.float32), 0.0).astype(jnp.bfloat16)
    row, column = iota((CAP, DEVICES * SUB), 0), iota((CAP, DEVICES * SUB), 1)
    part = column & (SUB - 1)
    weight = jnp.where(part == 0, CODE_BASE, jnp.where(part == 1, 1, 0))
    weight = jnp.where(column >> 6 == row, weight, 0)
    code = matmul(weight.astype(jnp.float32).astype(jnp.bfloat16), codes).astype(jnp.int32)
    code = jnp.concatenate([code[k:k + 1] for k in range(CAP)], axis=1)
    keep_base = CODE_BASE * CODE_KEEP
    owner = (code & (keep_base - 1)) - CODE_BASE
    kept = jnp.where(code >= keep_base, owner, -1)
    rows = jnp.concatenate(
        [arrived[:, c * PER:(c + 1) * PER].reshape(SLOTS, LANES) for c in range(WIDTH // LANES)], axis=1
    )
    labels = [iota((count, SLOTS), 0) + start for start, count, _ in CHUNKS]
    sums = [matmul(as_bf16(label == kept), rows) for label in labels]
    stores, products = [], None
    for k, (start, _, real) in enumerate(CHUNKS):
        inv_scale = lax.rsqrt(
            jnp.sum(sums[k] * sums[k], axis=1, keepdims=True) * (1.0 / WIDTH) + 1e-06
        ) / math.sqrt(WIDTH)
        unit = (sums[k] * inv_scale).astype(jnp.bfloat16)
        centroids[pl.ds(start, real)] = unit[:real]
        if k == len(CHUNKS) - 1:
            stores.append(pltpu.make_async_copy(centroids, centroids_hbm, out_sem.at[0]))
            stores[-1].start()
        similar = matmul(unit, rows, NT)
        part = jnp.sum(jnp.where(labels[k] == owner, similar, 0.0), axis=0, keepdims=True)
        products = part if products is None else products + part
    spread = jnp.concatenate(
        [jnp.broadcast_to(products[:, k * LANES:(k + 1) * LANES], (GROUP, LANES)) for k in range(CAP)], axis=0
    )
    square = (DEVICES, LANES)
    products_ref[...] = jnp.where(iota(square, 0) & (GROUP - 1) == iota(square, 1) >> 3, spread, 0.0)
    stores.append(pltpu.make_async_copy(products_ref, products_hbm, out_sem.at[1]))
    stores[-1].start()
    load.wait()
    total = None
    for c in range(WIDTH // LANES):
        piece = emb[:, c * LANES:(c + 1) * LANES].astype(jnp.float32)
        total = piece * piece if total is None else total + piece * piece
    squares = jnp.sum(total.T, axis=0, keepdims=True)
    scale_ref[...] = lax.rsqrt(squares * (1.0 / WIDTH) + 1e-06) / math.sqrt(WIDTH)
    for store in stores:
        store.wait()


def middle(arrived, embeddings):
    vmem = pl.BlockSpec(memory_space=pltpu.VMEM)
    hbm = pl.BlockSpec(memory_space=pl.ANY)
    return pl.pallas_call(
        middle_kernel,
        out_shape=(
            jax.ShapeDtypeStruct((CLUSTER_DEV, WIDTH), jnp.bfloat16),
            jax.ShapeDtypeStruct((DEVICES, LANES), jnp.float32),
            jax.ShapeDtypeStruct((1, ROWS), jnp.float32),
        ),
        in_specs=[vmem, hbm],
        out_specs=(hbm, hbm, vmem),
        scratch_shapes=[
            pltpu.VMEM((ROWS, WIDTH), jnp.bfloat16),
            pltpu.VMEM((CLUSTER_DEV, WIDTH), jnp.bfloat16),
            pltpu.VMEM((DEVICES, LANES), jnp.float32),
            pltpu.SemaphoreType.DMA,
            pltpu.SemaphoreType.DMA((2,)),
        ],
        compiler_params=pltpu.CompilerParams(vmem_limit_bytes=VMEM_LIMIT),
    )(arrived, embeddings)


def final_kernel(returned_ref, slot_ref, scale_ref, scores_ref):
    slot = slot_ref[...]
    hits = as_bf16(iota((DEVICES, ROWS), 0) == slot >> 3)
    back = jnp.sum(returned_ref[...].T.reshape(GROUP, CAP, DEVICES), axis=0)
    total = None
    for part in split3(back):
        term = matmul(part, hits)
        total = term if total is None else total + term
    chosen = jnp.where(iota((CAP, ROWS), 0) == slot & (CAP - 1), total, 0.0)
    scores_ref[...] = jnp.sum(chosen, axis=0, keepdims=True) * scale_ref[...]


def final(returned, slot, scale):
    vmem = pl.BlockSpec(memory_space=pltpu.VMEM)
    return pl.pallas_call(
        final_kernel,
        out_shape=jax.ShapeDtypeStruct((1, ROWS), jnp.float32),
        in_specs=[vmem] * 3,
        out_specs=vmem,
        compiler_params=pltpu.CompilerParams(vmem_limit_bytes=16 * 1024 * 1024),
    )(returned, slot, scale)


def body(embeddings, cluster_ids, keep_flags):
    outgoing, slot = pack(cluster_ids.reshape(1, ROWS), keep_flags.reshape(1, ROWS), embeddings)
    arrived = lax.all_to_all(outgoing, AXES, split_axis=0, concat_axis=0, tiled=True)
    centroids, products, row_scale = middle(arrived, embeddings)
    returned = lax.all_to_all(products, AXES, split_axis=0, concat_axis=0, tiled=True)
    scores = final(returned, slot, row_scale)
    return (centroids, scores.reshape(ROWS))


def solution(mesh):
    in_specs = (P(AXES, None), P(AXES), P(AXES))
    out_specs = (P(AXES, None), P(AXES))
    return jax.shard_map(body, mesh=mesh, in_specs=in_specs, out_specs=out_specs, check_vma=False)
```

```python
import math

import jax
import jax.numpy as jnp
from jax import lax
from jax.experimental import pallas as pl
from jax.experimental.pallas import tpu as pltpu
from jax.sharding import PartitionSpec as P

AXES = ("doc", "own")
CLUSTER_DEV = 392
CHUNKS = ((0, 208, 208), (208, 192, 184))
DEVICES = 128
CAP = 8
SLOTS = DEVICES * CAP
ROWS = 512
WIDTH = 768
LANES = 128
SUB = 4
PER = CAP // SUB
DATA_TILES = WIDTH // LANES * PER
GROUP = LANES // CAP
CODE_BASE = 16
CODE_KEEP = 32
PARTS = (256, 256, 256, 128, 128)
PACK_VMEM = 40 * 1024 * 1024
VMEM_LIMIT = 48 * 1024 * 1024

NN = (((1,), (0,)), ((), ()))
NT = (((1,), (1,)), ((), ()))


def iota(shape, axis):
    return lax.broadcasted_iota(jnp.int32, shape, axis)


def matmul(a, b, dims=NN):
    return lax.dot_general(a, b, dims, preferred_element_type=jnp.float32)


def as_bf16(mask):
    return jnp.where(mask, 1.0, 0.0).astype(jnp.bfloat16)


def split3(x):
    high = x.astype(jnp.bfloat16)
    rest = x - high.astype(jnp.float32)
    middle = rest.astype(jnp.bfloat16)
    low = (rest - middle.astype(jnp.float32)).astype(jnp.bfloat16)
    return high, middle, low


def owner_device(ids):
    return ((ids >> 3) * 5350) >> 18


def pack_kernel(
    ids_hbm, keep_hbm, emb_hbm, out_ref, slot_ref, ids_ref, keep_ref, emb, in_sem
):
    loads = [
        pltpu.make_async_copy(source, kept, in_sem.at[k])
        for k, (source, kept) in enumerate(((ids_hbm, ids_ref), (keep_hbm, keep_ref), (emb_hbm, emb)))
    ]
    for load in loads:
        load.start()
    loads[0].wait()
    loads[1].wait()
    ids = ids_ref[...]
    target = owner_device(ids)
    local = ids - target * CLUSTER_DEV
    hits = iota((DEVICES, ROWS), 0) == target
    hits_bf = as_bf16(hits)
    earlier = as_bf16(iota((LANES, LANES), 0) < iota((LANES, LANES), 1))
    every = jnp.ones((LANES, LANES), jnp.bfloat16)
    before, offset = [], None
    blocks = ROWS // LANES
    for k in range(blocks):
        block = hits_bf[:, k * LANES:(k + 1) * LANES]
        count = matmul(block, earlier)
        before.append(count if offset is None else count + offset)
        if k < blocks - 1:
            total = matmul(block, every)
            offset = total if offset is None else offset + total
    counts = jnp.concatenate(before, axis=1)
    position = jnp.sum(jnp.where(hits, counts, 0.0), axis=0, keepdims=True).astype(jnp.int32)
    slot = target * CAP + position
    slot_ref[...] = slot
    at_slot = iota((LANES, ROWS), 0) & (CAP - 1) == position
    upper = (local >> 4) + 1 + CODE_KEEP * keep_ref[...]
    lower = local & (CODE_BASE - 1)
    coded = [
        matmul(hits_bf, jnp.where(at_slot, part, 0).astype(jnp.float32).astype(jnp.bfloat16), NT)
        for part in (upper, lower)
    ]
    which = iota((DEVICES, SUB, LANES), 1)
    tile = jnp.where(which == 1, coded[1][:, None, :], 0.0)
    tile = jnp.where(which == 0, coded[0][:, None, :], tile)
    out_ref[:, DATA_TILES] = tile.astype(jnp.bfloat16)
    loads[2].wait()
    first = 0
    for k, count in enumerate(PARTS):
        place = as_bf16(iota((count, ROWS), 0) + first == slot)
        block = matmul(place, emb[...])
        peers = pl.ds(first // CAP, count // CAP)
        for c in range(WIDTH // LANES):
            piece = block[:, c * LANES:(c + 1) * LANES].reshape(count // CAP, PER, SUB, LANES)
            out_ref[peers, c * PER:(c + 1) * PER] = piece.astype(jnp.bfloat16)
        first += count


def pack(ids, keep, embeddings):
    vmem = pl.BlockSpec(memory_space=pltpu.VMEM)
    hbm = pl.BlockSpec(memory_space=pl.ANY)
    operands = [pltpu.with_memory_space_constraint(x, pltpu.HBM) for x in (ids, keep, embeddings)]
    return pl.pallas_call(
        pack_kernel,
        out_shape=(
            jax.ShapeDtypeStruct((DEVICES, DATA_TILES + 1, SUB, LANES), jnp.bfloat16),
            jax.ShapeDtypeStruct((1, ROWS), jnp.int32),
        ),
        in_specs=[hbm] * 3,
        out_specs=(vmem, vmem),
        scratch_shapes=[
            pltpu.VMEM((1, ROWS), jnp.int32),
            pltpu.VMEM((1, ROWS), jnp.int32),
            pltpu.VMEM((ROWS, WIDTH), jnp.bfloat16),
            pltpu.SemaphoreType.DMA((3,)),
        ],
        compiler_params=pltpu.CompilerParams(vmem_limit_bytes=PACK_VMEM),
    )(*operands)


def middle_kernel(
    arrived, emb_hbm, centroids_hbm, products_hbm, scale_ref, emb, centroids, products_ref, in_sem, out_sem
):
    load = pltpu.make_async_copy(emb_hbm, emb, in_sem)
    load.start()
    flat = (DEVICES * SUB, LANES)
    codes = arrived[:, DATA_TILES].reshape(flat)
    place = (iota(flat, 0) >> 2) & (GROUP - 1) == iota(flat, 1) >> 3
    codes = jnp.where(place, codes.astype(jnp.float32), 0.0).astype(jnp.bfloat16)
    row, column = iota((CAP, DEVICES * SUB), 0), iota((CAP, DEVICES * SUB), 1)
    part = column & (SUB - 1)
    weight = jnp.where(part == 0, CODE_BASE, jnp.where(part == 1, 1, 0))
    weight = jnp.where(column >> 6 == row, weight, 0)
    code = matmul(weight.astype(jnp.float32).astype(jnp.bfloat16), codes).astype(jnp.int32)
    code = jnp.concatenate([code[k:k + 1] for k in range(CAP)], axis=1)
    keep_base = CODE_BASE * CODE_KEEP
    owner = (code & (keep_base - 1)) - CODE_BASE
    kept = jnp.where(code >= keep_base, owner, -1)
    rows = jnp.concatenate(
        [arrived[:, c * PER:(c + 1) * PER].reshape(SLOTS, LANES) for c in range(WIDTH // LANES)], axis=1
    )
    labels = [iota((count, SLOTS), 0) + start for start, count, _ in CHUNKS]
    sums = [matmul(as_bf16(label == kept), rows) for label in labels]
    stores, products = [], None
    for k, (start, _, real) in enumerate(CHUNKS):
        inv_scale = lax.rsqrt(
            jnp.sum(sums[k] * sums[k], axis=1, keepdims=True) * (1.0 / WIDTH) + 1e-06
        ) / math.sqrt(WIDTH)
        unit = (sums[k] * inv_scale).astype(jnp.bfloat16)
        centroids[pl.ds(start, real)] = unit[:real]
        if k == len(CHUNKS) - 1:
            stores.append(pltpu.make_async_copy(centroids, centroids_hbm, out_sem.at[0]))
            stores[-1].start()
        similar = matmul(unit, rows, NT)
        part = jnp.sum(jnp.where(labels[k] == owner, similar, 0.0), axis=0, keepdims=True)
        products = part if products is None else products + part
    spread = jnp.concatenate(
        [jnp.broadcast_to(products[:, k * LANES:(k + 1) * LANES], (GROUP, LANES)) for k in range(CAP)], axis=0
    )
    square = (DEVICES, LANES)
    products_ref[...] = jnp.where(iota(square, 0) & (GROUP - 1) == iota(square, 1) >> 3, spread, 0.0)
    stores.append(pltpu.make_async_copy(products_ref, products_hbm, out_sem.at[1]))
    stores[-1].start()
    load.wait()
    total = None
    for c in range(WIDTH // LANES):
        piece = emb[:, c * LANES:(c + 1) * LANES].astype(jnp.float32)
        total = piece * piece if total is None else total + piece * piece
    squares = jnp.sum(total.T, axis=0, keepdims=True)
    scale_ref[...] = lax.rsqrt(squares * (1.0 / WIDTH) + 1e-06) / math.sqrt(WIDTH)
    for store in stores:
        store.wait()


def middle(arrived, embeddings):
    vmem = pl.BlockSpec(memory_space=pltpu.VMEM)
    hbm = pl.BlockSpec(memory_space=pl.ANY)
    return pl.pallas_call(
        middle_kernel,
        out_shape=(
            jax.ShapeDtypeStruct((CLUSTER_DEV, WIDTH), jnp.bfloat16),
            jax.ShapeDtypeStruct((DEVICES, LANES), jnp.float32),
            jax.ShapeDtypeStruct((1, ROWS), jnp.float32),
        ),
        in_specs=[vmem, hbm],
        out_specs=(hbm, hbm, vmem),
        scratch_shapes=[
            pltpu.VMEM((ROWS, WIDTH), jnp.bfloat16),
            pltpu.VMEM((CLUSTER_DEV, WIDTH), jnp.bfloat16),
            pltpu.VMEM((DEVICES, LANES), jnp.float32),
            pltpu.SemaphoreType.DMA,
            pltpu.SemaphoreType.DMA((2,)),
        ],
        compiler_params=pltpu.CompilerParams(vmem_limit_bytes=VMEM_LIMIT),
    )(arrived, embeddings)


def final_kernel(returned_ref, slot_ref, scale_ref, scores_ref):
    slot = slot_ref[...]
    hits = as_bf16(iota((DEVICES, ROWS), 0) == slot >> 3)
    back = jnp.sum(returned_ref[...].T.reshape(GROUP, CAP, DEVICES), axis=0)
    total = None
    for part in split3(back):
        term = matmul(part, hits)
        total = term if total is None else total + term
    chosen = jnp.where(iota((CAP, ROWS), 0) == slot & (CAP - 1), total, 0.0)
    scores_ref[...] = jnp.sum(chosen, axis=0, keepdims=True) * scale_ref[...]


def final(returned, slot, scale):
    vmem = pl.BlockSpec(memory_space=pltpu.VMEM)
    return pl.pallas_call(
        final_kernel,
        out_shape=jax.ShapeDtypeStruct((1, ROWS), jnp.float32),
        in_specs=[vmem] * 3,
        out_specs=vmem,
        compiler_params=pltpu.CompilerParams(vmem_limit_bytes=16 * 1024 * 1024),
    )(returned, slot, scale)


def body(embeddings, cluster_ids, keep_flags):
    outgoing, slot = pack(cluster_ids.reshape(1, ROWS), keep_flags.reshape(1, ROWS), embeddings)
    arrived = lax.all_to_all(outgoing, AXES, split_axis=0, concat_axis=0, tiled=True)
    centroids, products, row_scale = middle(arrived, embeddings)
    returned = lax.all_to_all(products, AXES, split_axis=0, concat_axis=0, tiled=True)
    scores = final(returned, slot, row_scale)
    return (centroids, scores.reshape(ROWS))


def solution(mesh):
    in_specs = (P(AXES, None), P(AXES), P(AXES))
    out_specs = (P(AXES, None), P(AXES))
    return jax.shard_map(body, mesh=mesh, in_specs=in_specs, out_specs=out_specs, check_vma=False)
```

```python
import math

import jax
import jax.numpy as jnp
from jax import lax
from jax.experimental import pallas as pl
from jax.experimental.pallas import tpu as pltpu
from jax.sharding import PartitionSpec as P

AXES = ("doc", "own")
CLUSTER_DEV = 392
CHUNKS = ((0, 208, 208), (208, 192, 184))
DEVICES = 128
CAP = 8
SLOTS = DEVICES * CAP
ROWS = 512
WIDTH = 768
LANES = 128
SUB = 4
PER = CAP // SUB
DATA_TILES = WIDTH // LANES * PER
GROUP = LANES // CAP
CODE_BASE = 16
CODE_KEEP = 32
PARTS = (256, 256, 256, 256)
PACK_VMEM = 40 * 1024 * 1024
VMEM_LIMIT = 48 * 1024 * 1024

NN = (((1,), (0,)), ((), ()))
NT = (((1,), (1,)), ((), ()))


def iota(shape, axis):
    return lax.broadcasted_iota(jnp.int32, shape, axis)


def matmul(a, b, dims=NN):
    return lax.dot_general(a, b, dims, preferred_element_type=jnp.float32)


def as_bf16(mask):
    return jnp.where(mask, 1.0, 0.0).astype(jnp.bfloat16)


def split3(x):
    high = x.astype(jnp.bfloat16)
    rest = x - high.astype(jnp.float32)
    middle = rest.astype(jnp.bfloat16)
    low = (rest - middle.astype(jnp.float32)).astype(jnp.bfloat16)
    return high, middle, low


def owner_device(ids):
    return ((ids >> 3) * 5350) >> 18


def pack_kernel(
    ids_hbm, keep_hbm, emb_hbm, out_ref, slot_ref, ids_ref, keep_ref, emb, in_sem
):
    loads = [
        pltpu.make_async_copy(source, kept, in_sem.at[k])
        for k, (source, kept) in enumerate(((ids_hbm, ids_ref), (keep_hbm, keep_ref), (emb_hbm, emb)))
    ]
    for load in loads:
        load.start()
    loads[0].wait()
    loads[1].wait()
    ids = ids_ref[...]
    target = owner_device(ids)
    local = ids - target * CLUSTER_DEV
    hits = iota((DEVICES, ROWS), 0) == target
    hits_bf = as_bf16(hits)
    earlier = as_bf16(iota((LANES, LANES), 0) < iota((LANES, LANES), 1))
    every = jnp.ones((LANES, LANES), jnp.bfloat16)
    before, offset = [], None
    blocks = ROWS // LANES
    for k in range(blocks):
        block = hits_bf[:, k * LANES:(k + 1) * LANES]
        count = matmul(block, earlier)
        before.append(count if offset is None else count + offset)
        if k < blocks - 1:
            total = matmul(block, every)
            offset = total if offset is None else offset + total
    counts = jnp.concatenate(before, axis=1)
    position = jnp.sum(jnp.where(hits, counts, 0.0), axis=0, keepdims=True).astype(jnp.int32)
    slot = target * CAP + position
    slot_ref[...] = slot
    at_slot = iota((LANES, ROWS), 0) & (CAP - 1) == position
    upper = (local >> 4) + 1 + CODE_KEEP * keep_ref[...]
    lower = local & (CODE_BASE - 1)
    coded = [
        matmul(hits_bf, jnp.where(at_slot, part, 0).astype(jnp.float32).astype(jnp.bfloat16), NT)
        for part in (upper, lower)
    ]
    which = iota((DEVICES, SUB, LANES), 1)
    tile = jnp.where(which == 1, coded[1][:, None, :], 0.0)
    tile = jnp.where(which == 0, coded[0][:, None, :], tile)
    out_ref[:, DATA_TILES] = tile.astype(jnp.bfloat16)
    loads[2].wait()
    first = 0
    for k, count in enumerate(PARTS):
        place = as_bf16(iota((count, ROWS), 0) + first == slot)
        block = matmul(place, emb[...])
        peers = pl.ds(first // CAP, count // CAP)
        for c in range(WIDTH // LANES):
            piece = block[:, c * LANES:(c + 1) * LANES].reshape(count // CAP, PER, SUB, LANES)
            out_ref[peers, c * PER:(c + 1) * PER] = piece.astype(jnp.bfloat16)
        first += count


def pack(ids, keep, embeddings):
    vmem = pl.BlockSpec(memory_space=pltpu.VMEM)
    hbm = pl.BlockSpec(memory_space=pl.ANY)
    operands = [pltpu.with_memory_space_constraint(x, pltpu.HBM) for x in (ids, keep, embeddings)]
    return pl.pallas_call(
        pack_kernel,
        out_shape=(
            jax.ShapeDtypeStruct((DEVICES, DATA_TILES + 1, SUB, LANES), jnp.bfloat16),
            jax.ShapeDtypeStruct((1, ROWS), jnp.int32),
        ),
        in_specs=[hbm] * 3,
        out_specs=(vmem, vmem),
        scratch_shapes=[
            pltpu.VMEM((1, ROWS), jnp.int32),
            pltpu.VMEM((1, ROWS), jnp.int32),
            pltpu.VMEM((ROWS, WIDTH), jnp.bfloat16),
            pltpu.SemaphoreType.DMA((3,)),
        ],
        compiler_params=pltpu.CompilerParams(vmem_limit_bytes=PACK_VMEM),
    )(*operands)


def middle_kernel(
    arrived, emb, centroids_ref, products_ref, scale_ref
):
    flat = (DEVICES * SUB, LANES)
    codes = arrived[:, DATA_TILES].reshape(flat)
    place = (iota(flat, 0) >> 2) & (GROUP - 1) == iota(flat, 1) >> 3
    codes = jnp.where(place, codes.astype(jnp.float32), 0.0).astype(jnp.bfloat16)
    row, column = iota((CAP, DEVICES * SUB), 0), iota((CAP, DEVICES * SUB), 1)
    part = column & (SUB - 1)
    weight = jnp.where(part == 0, CODE_BASE, jnp.where(part == 1, 1, 0))
    weight = jnp.where(column >> 6 == row, weight, 0)
    code = matmul(weight.astype(jnp.float32).astype(jnp.bfloat16), codes).astype(jnp.int32)
    code = jnp.concatenate([code[k:k + 1] for k in range(CAP)], axis=1)
    keep_base = CODE_BASE * CODE_KEEP
    owner = (code & (keep_base - 1)) - CODE_BASE
    kept = jnp.where(code >= keep_base, owner, -1)
    rows = jnp.concatenate(
        [arrived[:, c * PER:(c + 1) * PER].reshape(SLOTS, LANES) for c in range(WIDTH // LANES)], axis=1
    )
    labels = [iota((count, SLOTS), 0) + start for start, count, _ in CHUNKS]
    sums = [matmul(as_bf16(label == kept), rows) for label in labels]
    total = None
    for c in range(WIDTH // LANES):
        piece = emb[:, c * LANES:(c + 1) * LANES].astype(jnp.float32)
        total = piece * piece if total is None else total + piece * piece
    squares = jnp.sum(total.T, axis=0, keepdims=True)
    scale_ref[...] = lax.rsqrt(squares * (1.0 / WIDTH) + 1e-06) / math.sqrt(WIDTH)
    products = None
    for k, (start, _, real) in enumerate(CHUNKS):
        inv_scale = lax.rsqrt(
            jnp.sum(sums[k] * sums[k], axis=1, keepdims=True) * (1.0 / WIDTH) + 1e-06
        ) / math.sqrt(WIDTH)
        unit = (sums[k] * inv_scale).astype(jnp.bfloat16)
        centroids_ref[pl.ds(start, real)] = unit[:real]
        similar = matmul(unit, rows, NT)
        part = jnp.sum(jnp.where(labels[k] == owner, similar, 0.0), axis=0, keepdims=True)
        products = part if products is None else products + part
    spread = jnp.concatenate(
        [jnp.broadcast_to(products[:, k * LANES:(k + 1) * LANES], (GROUP, LANES)) for k in range(CAP)], axis=0
    )
    square = (DEVICES, LANES)
    products_ref[...] = jnp.where(iota(square, 0) & (GROUP - 1) == iota(square, 1) >> 3, spread, 0.0)


def middle(arrived, embeddings):
    vmem = pl.BlockSpec(memory_space=pltpu.VMEM)
    return pl.pallas_call(
        middle_kernel,
        out_shape=(
            jax.ShapeDtypeStruct((CLUSTER_DEV, WIDTH), jnp.bfloat16),
            jax.ShapeDtypeStruct((DEVICES, LANES), jnp.float32),
            jax.ShapeDtypeStruct((1, ROWS), jnp.float32),
        ),
        in_specs=[vmem, vmem],
        out_specs=(vmem, vmem, vmem),
        compiler_params=pltpu.CompilerParams(vmem_limit_bytes=VMEM_LIMIT),
    )(arrived, embeddings)


def final_kernel(
    returned_ref, slot_ref, scale_ref, centroids_ref, centroids_hbm, scores_hbm, scores, out_sem
):
    stores = [pltpu.make_async_copy(centroids_ref, centroids_hbm, out_sem.at[0])]
    stores[-1].start()
    slot = slot_ref[...]
    hits = as_bf16(iota((DEVICES, ROWS), 0) == slot >> 3)
    back = jnp.sum(returned_ref[...].T.reshape(GROUP, CAP, DEVICES), axis=0)
    total = None
    for part in split3(back):
        term = matmul(part, hits)
        total = term if total is None else total + term
    chosen = jnp.where(iota((CAP, ROWS), 0) == slot & (CAP - 1), total, 0.0)
    scores[...] = jnp.sum(chosen, axis=0, keepdims=True) * scale_ref[...]
    stores.append(pltpu.make_async_copy(scores, scores_hbm, out_sem.at[1]))
    stores[-1].start()
    for store in stores:
        store.wait()


def final(returned, slot, scale, centroids):
    vmem = pl.BlockSpec(memory_space=pltpu.VMEM)
    hbm = pl.BlockSpec(memory_space=pl.ANY)
    return pl.pallas_call(
        final_kernel,
        out_shape=(
            jax.ShapeDtypeStruct((CLUSTER_DEV, WIDTH), jnp.bfloat16),
            jax.ShapeDtypeStruct((1, ROWS), jnp.float32),
        ),
        in_specs=[vmem] * 4,
        out_specs=(hbm, hbm),
        scratch_shapes=[pltpu.VMEM((1, ROWS), jnp.float32), pltpu.SemaphoreType.DMA((2,))],
        compiler_params=pltpu.CompilerParams(vmem_limit_bytes=16 * 1024 * 1024),
    )(returned, slot, scale, centroids)


def body(embeddings, cluster_ids, keep_flags):
    outgoing, slot = pack(cluster_ids.reshape(1, ROWS), keep_flags.reshape(1, ROWS), embeddings)
    arrived = lax.all_to_all(outgoing, AXES, split_axis=0, concat_axis=0, tiled=True)
    centroids, products, row_scale = middle(arrived, embeddings)
    returned = lax.all_to_all(products, AXES, split_axis=0, concat_axis=0, tiled=True)
    centroids, scores = final(returned, slot, row_scale, centroids)
    return (centroids, scores.reshape(ROWS))


def solution(mesh):
    in_specs = (P(AXES, None), P(AXES), P(AXES))
    out_specs = (P(AXES, None), P(AXES))
    return jax.shard_map(body, mesh=mesh, in_specs=in_specs, out_specs=out_specs, check_vma=False)
```

```python
import math

import jax
import jax.numpy as jnp
from jax import lax
from jax.experimental import pallas as pl
from jax.experimental.pallas import tpu as pltpu
from jax.sharding import PartitionSpec as P

AXES = ("doc", "own")
CLUSTER_DEV = 392
CHUNKS = ((0, 208, 208), (208, 192, 184))
DEVICES = 128
CAP = 8
SLOTS = DEVICES * CAP
ROWS = 512
WIDTH = 768
LANES = 128
SUB = 4
PER = CAP // SUB
DATA_TILES = WIDTH // LANES * PER
GROUP = LANES // CAP
CODE_BASE = 16
CODE_KEEP = 32
PARTS = (256, 256, 256, 256)
PACK_VMEM = 40 * 1024 * 1024
VMEM_LIMIT = 48 * 1024 * 1024

NN = (((1,), (0,)), ((), ()))
NT = (((1,), (1,)), ((), ()))


def iota(shape, axis):
    return lax.broadcasted_iota(jnp.int32, shape, axis)


def matmul(a, b, dims=NN):
    return lax.dot_general(a, b, dims, preferred_element_type=jnp.float32)


def as_bf16(mask):
    return jnp.where(mask, 1.0, 0.0).astype(jnp.bfloat16)


def split3(x):
    high = x.astype(jnp.bfloat16)
    rest = x - high.astype(jnp.float32)
    middle = rest.astype(jnp.bfloat16)
    low = (rest - middle.astype(jnp.float32)).astype(jnp.bfloat16)
    return high, middle, low


def owner_device(ids):
    return ((ids >> 3) * 5350) >> 18


def pack_kernel(
    ids_hbm, keep_hbm, emb_hbm, out_ref, slot_ref, ids_ref, keep_ref, emb, in_sem
):
    loads = [
        pltpu.make_async_copy(source, kept, in_sem.at[k])
        for k, (source, kept) in enumerate(((ids_hbm, ids_ref), (keep_hbm, keep_ref), (emb_hbm, emb)))
    ]
    for load in loads:
        load.start()
    loads[0].wait()
    loads[1].wait()
    ids = ids_ref[...]
    target = owner_device(ids)
    local = ids - target * CLUSTER_DEV
    hits = iota((DEVICES, ROWS), 0) == target
    hits_bf = as_bf16(hits)
    earlier = as_bf16(iota((LANES, LANES), 0) < iota((LANES, LANES), 1))
    every = jnp.ones((LANES, LANES), jnp.bfloat16)
    before, offset = [], None
    blocks = ROWS // LANES
    for k in range(blocks):
        block = hits_bf[:, k * LANES:(k + 1) * LANES]
        count = matmul(block, earlier)
        before.append(count if offset is None else count + offset)
        if k < blocks - 1:
            total = matmul(block, every)
            offset = total if offset is None else offset + total
    counts = jnp.concatenate(before, axis=1)
    position = jnp.sum(jnp.where(hits, counts, 0.0), axis=0, keepdims=True).astype(jnp.int32)
    slot = target * CAP + position
    slot_ref[...] = slot
    at_slot = iota((LANES, ROWS), 0) & (CAP - 1) == position
    upper = (local >> 4) + 1 + CODE_KEEP * keep_ref[...]
    lower = local & (CODE_BASE - 1)
    coded = [
        matmul(hits_bf, jnp.where(at_slot, part, 0).astype(jnp.float32).astype(jnp.bfloat16), NT)
        for part in (upper, lower)
    ]
    which = iota((DEVICES, SUB, LANES), 1)
    tile = jnp.where(which == 1, coded[1][:, None, :], 0.0)
    tile = jnp.where(which == 0, coded[0][:, None, :], tile)
    out_ref[:, DATA_TILES] = tile.astype(jnp.bfloat16)
    loads[2].wait()
    first = 0
    for k, count in enumerate(PARTS):
        place = as_bf16(iota((count, ROWS), 0) + first == slot)
        block = matmul(place, emb[...])
        peers = pl.ds(first // CAP, count // CAP)
        for c in range(WIDTH // LANES):
            piece = block[:, c * LANES:(c + 1) * LANES].reshape(count // CAP, PER, SUB, LANES)
            out_ref[peers, c * PER:(c + 1) * PER] = piece.astype(jnp.bfloat16)
        first += count


def pack(ids, keep, embeddings):
    vmem = pl.BlockSpec(memory_space=pltpu.VMEM)
    hbm = pl.BlockSpec(memory_space=pl.ANY)
    operands = [pltpu.with_memory_space_constraint(x, pltpu.HBM) for x in (ids, keep, embeddings)]
    return pl.pallas_call(
        pack_kernel,
        out_shape=(
            jax.ShapeDtypeStruct((DEVICES, DATA_TILES + 1, SUB, LANES), jnp.bfloat16),
            jax.ShapeDtypeStruct((1, ROWS), jnp.int32),
        ),
        in_specs=[hbm] * 3,
        out_specs=(vmem, vmem),
        scratch_shapes=[
            pltpu.VMEM((1, ROWS), jnp.int32),
            pltpu.VMEM((1, ROWS), jnp.int32),
            pltpu.VMEM((ROWS, WIDTH), jnp.bfloat16),
            pltpu.SemaphoreType.DMA((3,)),
        ],
        compiler_params=pltpu.CompilerParams(vmem_limit_bytes=PACK_VMEM),
    )(*operands)


def middle_kernel(
    arrived, emb, centroids_ref, products_ref, scale_ref
):
    flat = (DEVICES * SUB, LANES)
    codes = arrived[:, DATA_TILES].reshape(flat)
    place = (iota(flat, 0) >> 2) & (GROUP - 1) == iota(flat, 1) >> 3
    codes = jnp.where(place, codes.astype(jnp.float32), 0.0).astype(jnp.bfloat16)
    row, column = iota((CAP, DEVICES * SUB), 0), iota((CAP, DEVICES * SUB), 1)
    part = column & (SUB - 1)
    weight = jnp.where(part == 0, CODE_BASE, jnp.where(part == 1, 1, 0))
    weight = jnp.where(column >> 6 == row, weight, 0)
    code = matmul(weight.astype(jnp.float32).astype(jnp.bfloat16), codes).astype(jnp.int32)
    code = jnp.concatenate([code[k:k + 1] for k in range(CAP)], axis=1)
    keep_base = CODE_BASE * CODE_KEEP
    owner = (code & (keep_base - 1)) - CODE_BASE
    kept = jnp.where(code >= keep_base, owner, -1)
    rows = jnp.concatenate(
        [arrived[:, c * PER:(c + 1) * PER].reshape(SLOTS, LANES) for c in range(WIDTH // LANES)], axis=1
    )
    labels = [iota((count, SLOTS), 0) + start for start, count, _ in CHUNKS]
    sums = [matmul(as_bf16(label == kept), rows) for label in labels]
    total = None
    for c in range(WIDTH // LANES):
        piece = emb[:, c * LANES:(c + 1) * LANES].astype(jnp.float32)
        total = piece * piece if total is None else total + piece * piece
    squares = jnp.sum(total.T, axis=0, keepdims=True)
    scale_ref[...] = lax.rsqrt(squares * (1.0 / WIDTH) + 1e-06) / math.sqrt(WIDTH)
    products = None
    for k, (start, _, real) in enumerate(CHUNKS):
        inv_scale = lax.rsqrt(
            jnp.sum(sums[k] * sums[k], axis=1, keepdims=True) * (1.0 / WIDTH) + 1e-06
        ) / math.sqrt(WIDTH)
        unit = (sums[k] * inv_scale).astype(jnp.bfloat16)
        centroids_ref[pl.ds(start, real)] = unit[:real]
        similar = matmul(unit, rows, NT)
        part = jnp.sum(jnp.where(labels[k] == owner, similar, 0.0), axis=0, keepdims=True)
        products = part if products is None else products + part
    spread = jnp.concatenate(
        [jnp.broadcast_to(products[:, k * LANES:(k + 1) * LANES], (GROUP, LANES)) for k in range(CAP)], axis=0
    )
    square = (DEVICES, LANES)
    products_ref[...] = jnp.where(iota(square, 0) & (GROUP - 1) == iota(square, 1) >> 3, spread, 0.0)


def middle(arrived, embeddings):
    vmem = pl.BlockSpec(memory_space=pltpu.VMEM)
    return pl.pallas_call(
        middle_kernel,
        out_shape=(
            jax.ShapeDtypeStruct((CLUSTER_DEV, WIDTH), jnp.bfloat16),
            jax.ShapeDtypeStruct((DEVICES, LANES), jnp.float32),
            jax.ShapeDtypeStruct((1, ROWS), jnp.float32),
        ),
        in_specs=[vmem, vmem],
        out_specs=(vmem, vmem, vmem),
        compiler_params=pltpu.CompilerParams(vmem_limit_bytes=VMEM_LIMIT),
    )(arrived, embeddings)


def final_kernel(
    returned_ref, slot_ref, scale_ref, centroids_ref, centroids_hbm, scores_hbm, scores, out_sem
):
    stores = [pltpu.make_async_copy(centroids_ref, centroids_hbm, out_sem.at[0])]
    stores[-1].start()
    slot = slot_ref[...]
    hits = as_bf16(iota((DEVICES, ROWS), 0) == slot >> 3)
    back = jnp.sum(returned_ref[...].T.reshape(GROUP, CAP, DEVICES), axis=0)
    parts = matmul(jnp.concatenate(split3(back), axis=0), hits)
    total = parts[:CAP] + parts[CAP:2 * CAP] + parts[2 * CAP:]
    chosen = jnp.where(iota((CAP, ROWS), 0) == slot & (CAP - 1), total, 0.0)
    scores[...] = jnp.sum(chosen, axis=0, keepdims=True) * scale_ref[...]
    stores.append(pltpu.make_async_copy(scores, scores_hbm, out_sem.at[1]))
    stores[-1].start()
    for store in stores:
        store.wait()


def final(returned, slot, scale, centroids):
    vmem = pl.BlockSpec(memory_space=pltpu.VMEM)
    hbm = pl.BlockSpec(memory_space=pl.ANY)
    return pl.pallas_call(
        final_kernel,
        out_shape=(
            jax.ShapeDtypeStruct((CLUSTER_DEV, WIDTH), jnp.bfloat16),
            jax.ShapeDtypeStruct((1, ROWS), jnp.float32),
        ),
        in_specs=[vmem] * 4,
        out_specs=(hbm, hbm),
        scratch_shapes=[pltpu.VMEM((1, ROWS), jnp.float32), pltpu.SemaphoreType.DMA((2,))],
        compiler_params=pltpu.CompilerParams(vmem_limit_bytes=16 * 1024 * 1024),
    )(returned, slot, scale, centroids)


def body(embeddings, cluster_ids, keep_flags):
    outgoing, slot = pack(cluster_ids.reshape(1, ROWS), keep_flags.reshape(1, ROWS), embeddings)
    arrived = lax.all_to_all(outgoing, AXES, split_axis=0, concat_axis=0, tiled=True)
    centroids, products, row_scale = middle(arrived, embeddings)
    returned = lax.all_to_all(products, AXES, split_axis=0, concat_axis=0, tiled=True)
    centroids, scores = final(returned, slot, row_scale, centroids)
    return (centroids, scores.reshape(ROWS))


def solution(mesh):
    in_specs = (P(AXES, None), P(AXES), P(AXES))
    out_specs = (P(AXES, None), P(AXES))
    return jax.shard_map(body, mesh=mesh, in_specs=in_specs, out_specs=out_specs, check_vma=False)
```

```python
import math

import jax
import jax.numpy as jnp
from jax import lax
from jax.experimental import pallas as pl
from jax.experimental.pallas import tpu as pltpu
from jax.sharding import PartitionSpec as P

AXES = ("doc", "own")
CLUSTER_DEV = 392
CHUNKS = ((0, 192, 192), (192, 200, 200))
DEVICES = 128
CAP = 8
SLOTS = DEVICES * CAP
ROWS = 512
WIDTH = 768
LANES = 128
SUB = 4
PER = CAP // SUB
DATA_TILES = WIDTH // LANES * PER
GROUP = LANES // CAP
CODE_BASE = 16
CODE_KEEP = 32
PARTS = (256, 256, 256, 256)
PACK_VMEM = 40 * 1024 * 1024
VMEM_LIMIT = 48 * 1024 * 1024

NN = (((1,), (0,)), ((), ()))
NT = (((1,), (1,)), ((), ()))


def iota(shape, axis):
    return lax.broadcasted_iota(jnp.int32, shape, axis)


def matmul(a, b, dims=NN):
    return lax.dot_general(a, b, dims, preferred_element_type=jnp.float32)


def as_bf16(mask):
    return jnp.where(mask, 1.0, 0.0).astype(jnp.bfloat16)


def split3(x):
    high = x.astype(jnp.bfloat16)
    rest = x - high.astype(jnp.float32)
    middle = rest.astype(jnp.bfloat16)
    low = (rest - middle.astype(jnp.float32)).astype(jnp.bfloat16)
    return high, middle, low


def owner_device(ids):
    return ((ids >> 3) * 5350) >> 18


def pack_kernel(
    ids_hbm, keep_hbm, emb_hbm, out_ref, slot_ref, ids_ref, keep_ref, emb, in_sem
):
    loads = [
        pltpu.make_async_copy(source, kept, in_sem.at[k])
        for k, (source, kept) in enumerate(((ids_hbm, ids_ref), (keep_hbm, keep_ref), (emb_hbm, emb)))
    ]
    for load in loads:
        load.start()
    loads[0].wait()
    loads[1].wait()
    ids = ids_ref[...]
    target = owner_device(ids)
    local = ids - target * CLUSTER_DEV
    hits = iota((DEVICES, ROWS), 0) == target
    hits_bf = as_bf16(hits)
    earlier = as_bf16(iota((LANES, LANES), 0) < iota((LANES, LANES), 1))
    every = jnp.ones((LANES, LANES), jnp.bfloat16)
    before, offset = [], None
    blocks = ROWS // LANES
    for k in range(blocks):
        block = hits_bf[:, k * LANES:(k + 1) * LANES]
        count = matmul(block, earlier)
        before.append(count if offset is None else count + offset)
        if k < blocks - 1:
            total = matmul(block, every)
            offset = total if offset is None else offset + total
    counts = jnp.concatenate(before, axis=1)
    position = jnp.sum(jnp.where(hits, counts, 0.0), axis=0, keepdims=True).astype(jnp.int32)
    slot = target * CAP + position
    slot_ref[...] = slot
    at_slot = iota((LANES, ROWS), 0) & (CAP - 1) == position
    upper = (local >> 4) + 1 + CODE_KEEP * keep_ref[...]
    lower = local & (CODE_BASE - 1)
    coded = [
        matmul(hits_bf, jnp.where(at_slot, part, 0).astype(jnp.float32).astype(jnp.bfloat16), NT)
        for part in (upper, lower)
    ]
    which = iota((DEVICES, SUB, LANES), 1)
    tile = jnp.where(which == 1, coded[1][:, None, :], 0.0)
    tile = jnp.where(which == 0, coded[0][:, None, :], tile)
    out_ref[:, DATA_TILES] = tile.astype(jnp.bfloat16)
    loads[2].wait()
    first = 0
    for k, count in enumerate(PARTS):
        place = as_bf16(iota((count, ROWS), 0) + first == slot)
        block = matmul(place, emb[...])
        peers = pl.ds(first // CAP, count // CAP)
        for c in range(WIDTH // LANES):
            piece = block[:, c * LANES:(c + 1) * LANES].reshape(count // CAP, PER, SUB, LANES)
            out_ref[peers, c * PER:(c + 1) * PER] = piece.astype(jnp.bfloat16)
        first += count


def pack(ids, keep, embeddings):
    vmem = pl.BlockSpec(memory_space=pltpu.VMEM)
    hbm = pl.BlockSpec(memory_space=pl.ANY)
    operands = [pltpu.with_memory_space_constraint(x, pltpu.HBM) for x in (ids, keep, embeddings)]
    return pl.pallas_call(
        pack_kernel,
        out_shape=(
            jax.ShapeDtypeStruct((DEVICES, DATA_TILES + 1, SUB, LANES), jnp.bfloat16),
            jax.ShapeDtypeStruct((1, ROWS), jnp.int32),
        ),
        in_specs=[hbm] * 3,
        out_specs=(vmem, vmem),
        scratch_shapes=[
            pltpu.VMEM((1, ROWS), jnp.int32),
            pltpu.VMEM((1, ROWS), jnp.int32),
            pltpu.VMEM((ROWS, WIDTH), jnp.bfloat16),
            pltpu.SemaphoreType.DMA((3,)),
        ],
        compiler_params=pltpu.CompilerParams(vmem_limit_bytes=PACK_VMEM),
    )(*operands)


def middle_kernel(
    arrived, emb, centroids_ref, products_ref, scale_ref
):
    flat = (DEVICES * SUB, LANES)
    codes = arrived[:, DATA_TILES].reshape(flat)
    place = (iota(flat, 0) >> 2) & (GROUP - 1) == iota(flat, 1) >> 3
    codes = jnp.where(place, codes.astype(jnp.float32), 0.0).astype(jnp.bfloat16)
    row, column = iota((CAP, DEVICES * SUB), 0), iota((CAP, DEVICES * SUB), 1)
    part = column & (SUB - 1)
    weight = jnp.where(part == 0, CODE_BASE, jnp.where(part == 1, 1, 0))
    weight = jnp.where(column >> 6 == row, weight, 0)
    code = matmul(weight.astype(jnp.float32).astype(jnp.bfloat16), codes).astype(jnp.int32)
    code = jnp.concatenate([code[k:k + 1] for k in range(CAP)], axis=1)
    keep_base = CODE_BASE * CODE_KEEP
    owner = (code & (keep_base - 1)) - CODE_BASE
    kept = jnp.where(code >= keep_base, owner, -1)
    rows = jnp.concatenate(
        [arrived[:, c * PER:(c + 1) * PER].reshape(SLOTS, LANES) for c in range(WIDTH // LANES)], axis=1
    )
    labels = [iota((count, SLOTS), 0) + start for start, count, _ in CHUNKS]
    sums = [matmul(as_bf16(label == kept), rows) for label in labels]
    total = None
    for c in range(WIDTH // LANES):
        piece = emb[:, c * LANES:(c + 1) * LANES].astype(jnp.float32)
        total = piece * piece if total is None else total + piece * piece
    squares = jnp.sum(total.T, axis=0, keepdims=True)
    scale_ref[...] = lax.rsqrt(squares * (1.0 / WIDTH) + 1e-06) / math.sqrt(WIDTH)
    products = None
    for k, (start, _, real) in enumerate(CHUNKS):
        inv_scale = lax.rsqrt(
            jnp.sum(sums[k] * sums[k], axis=1, keepdims=True) * (1.0 / WIDTH) + 1e-06
        ) / math.sqrt(WIDTH)
        unit = (sums[k] * inv_scale).astype(jnp.bfloat16)
        centroids_ref[pl.ds(start, real)] = unit[:real]
        similar = matmul(unit, rows, NT)
        part = jnp.sum(jnp.where(labels[k] == owner, similar, 0.0), axis=0, keepdims=True)
        products = part if products is None else products + part
    spread = jnp.concatenate(
        [jnp.broadcast_to(products[:, k * LANES:(k + 1) * LANES], (GROUP, LANES)) for k in range(CAP)], axis=0
    )
    square = (DEVICES, LANES)
    products_ref[...] = jnp.where(iota(square, 0) & (GROUP - 1) == iota(square, 1) >> 3, spread, 0.0)


def middle(arrived, embeddings):
    vmem = pl.BlockSpec(memory_space=pltpu.VMEM)
    return pl.pallas_call(
        middle_kernel,
        out_shape=(
            jax.ShapeDtypeStruct((CLUSTER_DEV, WIDTH), jnp.bfloat16),
            jax.ShapeDtypeStruct((DEVICES, LANES), jnp.float32),
            jax.ShapeDtypeStruct((1, ROWS), jnp.float32),
        ),
        in_specs=[vmem, vmem],
        out_specs=(vmem, vmem, vmem),
        compiler_params=pltpu.CompilerParams(vmem_limit_bytes=VMEM_LIMIT),
    )(arrived, embeddings)


def final_kernel(
    returned_ref, slot_ref, scale_ref, centroids_ref, centroids_hbm, scores_hbm, scores, out_sem
):
    stores = [pltpu.make_async_copy(centroids_ref, centroids_hbm, out_sem.at[0])]
    stores[-1].start()
    slot = slot_ref[...]
    hits = as_bf16(iota((DEVICES, ROWS), 0) == slot >> 3)
    back = jnp.sum(returned_ref[...].T.reshape(GROUP, CAP, DEVICES), axis=0)
    parts = matmul(jnp.concatenate(split3(back), axis=0), hits)
    total = parts[:CAP] + parts[CAP:2 * CAP] + parts[2 * CAP:]
    chosen = jnp.where(iota((CAP, ROWS), 0) == slot & (CAP - 1), total, 0.0)
    scores[...] = jnp.sum(chosen, axis=0, keepdims=True) * scale_ref[...]
    stores.append(pltpu.make_async_copy(scores, scores_hbm, out_sem.at[1]))
    stores[-1].start()
    for store in stores:
        store.wait()


def final(returned, slot, scale, centroids):
    vmem = pl.BlockSpec(memory_space=pltpu.VMEM)
    hbm = pl.BlockSpec(memory_space=pl.ANY)
    return pl.pallas_call(
        final_kernel,
        out_shape=(
            jax.ShapeDtypeStruct((CLUSTER_DEV, WIDTH), jnp.bfloat16),
            jax.ShapeDtypeStruct((1, ROWS), jnp.float32),
        ),
        in_specs=[vmem] * 4,
        out_specs=(hbm, hbm),
        scratch_shapes=[pltpu.VMEM((1, ROWS), jnp.float32), pltpu.SemaphoreType.DMA((2,))],
        compiler_params=pltpu.CompilerParams(vmem_limit_bytes=16 * 1024 * 1024),
    )(returned, slot, scale, centroids)


def body(embeddings, cluster_ids, keep_flags):
    outgoing, slot = pack(cluster_ids.reshape(1, ROWS), keep_flags.reshape(1, ROWS), embeddings)
    arrived = lax.all_to_all(outgoing, AXES, split_axis=0, concat_axis=0, tiled=True)
    centroids, products, row_scale = middle(arrived, embeddings)
    returned = lax.all_to_all(products, AXES, split_axis=0, concat_axis=0, tiled=True)
    centroids, scores = final(returned, slot, row_scale, centroids)
    return (centroids, scores.reshape(ROWS))


def solution(mesh):
    in_specs = (P(AXES, None), P(AXES), P(AXES))
    out_specs = (P(AXES, None), P(AXES))
    return jax.shard_map(body, mesh=mesh, in_specs=in_specs, out_specs=out_specs, check_vma=False)
```

```python
import math

import jax
import jax.numpy as jnp
from jax import lax
from jax.experimental import pallas as pl
from jax.experimental.pallas import tpu as pltpu
from jax.sharding import PartitionSpec as P

AXES = ("doc", "own")
CLUSTER_DEV = 392
CHUNKS = ((0, 208, 208), (208, 184, 184))
DEVICES = 128
CAP = 8
SLOTS = DEVICES * CAP
ROWS = 512
WIDTH = 768
LANES = 128
SUB = 4
PER = CAP // SUB
DATA_TILES = WIDTH // LANES * PER
GROUP = LANES // CAP
CODE_BASE = 16
CODE_KEEP = 32
PARTS = (256, 256, 256, 256)
PACK_VMEM = 40 * 1024 * 1024
VMEM_LIMIT = 48 * 1024 * 1024

NN = (((1,), (0,)), ((), ()))
NT = (((1,), (1,)), ((), ()))


def iota(shape, axis):
    return lax.broadcasted_iota(jnp.int32, shape, axis)


def matmul(a, b, dims=NN):
    return lax.dot_general(a, b, dims, preferred_element_type=jnp.float32)


def as_bf16(mask):
    return jnp.where(mask, 1.0, 0.0).astype(jnp.bfloat16)


def split3(x):
    high = x.astype(jnp.bfloat16)
    rest = x - high.astype(jnp.float32)
    middle = rest.astype(jnp.bfloat16)
    low = (rest - middle.astype(jnp.float32)).astype(jnp.bfloat16)
    return high, middle, low


def owner_device(ids):
    return ((ids >> 3) * 5350) >> 18


def pack_kernel(
    ids_hbm, keep_hbm, emb_hbm, out_ref, slot_ref, ids_ref, keep_ref, emb, in_sem
):
    loads = [
        pltpu.make_async_copy(source, kept, in_sem.at[k])
        for k, (source, kept) in enumerate(((ids_hbm, ids_ref), (keep_hbm, keep_ref), (emb_hbm, emb)))
    ]
    for load in loads:
        load.start()
    loads[0].wait()
    loads[1].wait()
    ids = ids_ref[...]
    target = owner_device(ids)
    local = ids - target * CLUSTER_DEV
    hits = iota((DEVICES, ROWS), 0) == target
    hits_bf = as_bf16(hits)
    earlier = as_bf16(iota((LANES, LANES), 0) < iota((LANES, LANES), 1))
    every = jnp.ones((LANES, LANES), jnp.bfloat16)
    before, offset = [], None
    blocks = ROWS // LANES
    for k in range(blocks):
        block = hits_bf[:, k * LANES:(k + 1) * LANES]
        count = matmul(block, earlier)
        before.append(count if offset is None else count + offset)
        if k < blocks - 1:
            total = matmul(block, every)
            offset = total if offset is None else offset + total
    counts = jnp.concatenate(before, axis=1)
    position = jnp.sum(jnp.where(hits, counts, 0.0), axis=0, keepdims=True).astype(jnp.int32)
    slot = target * CAP + position
    slot_ref[...] = slot
    at_slot = iota((LANES, ROWS), 0) & (CAP - 1) == position
    upper = (local >> 4) + 1 + CODE_KEEP * keep_ref[...]
    lower = local & (CODE_BASE - 1)
    coded = [
        matmul(hits_bf, jnp.where(at_slot, part, 0).astype(jnp.float32).astype(jnp.bfloat16), NT)
        for part in (upper, lower)
    ]
    which = iota((DEVICES, SUB, LANES), 1)
    tile = jnp.where(which == 1, coded[1][:, None, :], 0.0)
    tile = jnp.where(which == 0, coded[0][:, None, :], tile)
    out_ref[:, DATA_TILES] = tile.astype(jnp.bfloat16)
    loads[2].wait()
    first = 0
    for k, count in enumerate(PARTS):
        place = as_bf16(iota((count, ROWS), 0) + first == slot)
        block = matmul(place, emb[...])
        peers = pl.ds(first // CAP, count // CAP)
        for c in range(WIDTH // LANES):
            piece = block[:, c * LANES:(c + 1) * LANES].reshape(count // CAP, PER, SUB, LANES)
            out_ref[peers, c * PER:(c + 1) * PER] = piece.astype(jnp.bfloat16)
        first += count


def pack(ids, keep, embeddings):
    vmem = pl.BlockSpec(memory_space=pltpu.VMEM)
    hbm = pl.BlockSpec(memory_space=pl.ANY)
    operands = [pltpu.with_memory_space_constraint(x, pltpu.HBM) for x in (ids, keep, embeddings)]
    return pl.pallas_call(
        pack_kernel,
        out_shape=(
            jax.ShapeDtypeStruct((DEVICES, DATA_TILES + 1, SUB, LANES), jnp.bfloat16),
            jax.ShapeDtypeStruct((1, ROWS), jnp.int32),
        ),
        in_specs=[hbm] * 3,
        out_specs=(vmem, vmem),
        scratch_shapes=[
            pltpu.VMEM((1, ROWS), jnp.int32),
            pltpu.VMEM((1, ROWS), jnp.int32),
            pltpu.VMEM((ROWS, WIDTH), jnp.bfloat16),
            pltpu.SemaphoreType.DMA((3,)),
        ],
        compiler_params=pltpu.CompilerParams(vmem_limit_bytes=PACK_VMEM),
    )(*operands)


def middle_kernel(
    arrived, emb, centroids_ref, products_ref, scale_ref
):
    flat = (DEVICES * SUB, LANES)
    codes = arrived[:, DATA_TILES].reshape(flat)
    place = (iota(flat, 0) >> 2) & (GROUP - 1) == iota(flat, 1) >> 3
    codes = jnp.where(place, codes.astype(jnp.float32), 0.0).astype(jnp.bfloat16)
    row, column = iota((CAP, DEVICES * SUB), 0), iota((CAP, DEVICES * SUB), 1)
    part = column & (SUB - 1)
    weight = jnp.where(part == 0, CODE_BASE, jnp.where(part == 1, 1, 0))
    weight = jnp.where(column >> 6 == row, weight, 0)
    code = matmul(weight.astype(jnp.float32).astype(jnp.bfloat16), codes).astype(jnp.int32)
    code = jnp.concatenate([code[k:k + 1] for k in range(CAP)], axis=1)
    keep_base = CODE_BASE * CODE_KEEP
    owner = (code & (keep_base - 1)) - CODE_BASE
    kept = jnp.where(code >= keep_base, owner, -1)
    rows = jnp.concatenate(
        [arrived[:, c * PER:(c + 1) * PER].reshape(SLOTS, LANES) for c in range(WIDTH // LANES)], axis=1
    )
    labels = [iota((count, SLOTS), 0) + start for start, count, _ in CHUNKS]
    sums = [matmul(as_bf16(label == kept), rows) for label in labels]
    total = None
    for c in range(WIDTH // LANES):
        piece = emb[:, c * LANES:(c + 1) * LANES].astype(jnp.float32)
        total = piece * piece if total is None else total + piece * piece
    squares = jnp.sum(total.T, axis=0, keepdims=True)
    scale_ref[...] = lax.rsqrt(squares * (1.0 / WIDTH) + 1e-06) / math.sqrt(WIDTH)
    products = None
    for k, (start, _, real) in enumerate(CHUNKS):
        inv_scale = lax.rsqrt(
            jnp.sum(sums[k] * sums[k], axis=1, keepdims=True) * (1.0 / WIDTH) + 1e-06
        ) / math.sqrt(WIDTH)
        unit = (sums[k] * inv_scale).astype(jnp.bfloat16)
        centroids_ref[pl.ds(start, real)] = unit[:real]
        similar = matmul(unit, rows, NT)
        part = jnp.sum(jnp.where(labels[k] == owner, similar, 0.0), axis=0, keepdims=True)
        products = part if products is None else products + part
    spread = jnp.concatenate(
        [jnp.broadcast_to(products[:, k * LANES:(k + 1) * LANES], (GROUP, LANES)) for k in range(CAP)], axis=0
    )
    square = (DEVICES, LANES)
    products_ref[...] = jnp.where(iota(square, 0) & (GROUP - 1) == iota(square, 1) >> 3, spread, 0.0)


def middle(arrived, embeddings):
    vmem = pl.BlockSpec(memory_space=pltpu.VMEM)
    return pl.pallas_call(
        middle_kernel,
        out_shape=(
            jax.ShapeDtypeStruct((CLUSTER_DEV, WIDTH), jnp.bfloat16),
            jax.ShapeDtypeStruct((DEVICES, LANES), jnp.float32),
            jax.ShapeDtypeStruct((1, ROWS), jnp.float32),
        ),
        in_specs=[vmem, vmem],
        out_specs=(vmem, vmem, vmem),
        compiler_params=pltpu.CompilerParams(vmem_limit_bytes=VMEM_LIMIT),
    )(arrived, embeddings)


def final_kernel(
    returned_ref, slot_ref, scale_ref, centroids_ref, centroids_hbm, scores_hbm, scores, out_sem
):
    stores = [pltpu.make_async_copy(centroids_ref, centroids_hbm, out_sem.at[0])]
    stores[-1].start()
    slot = slot_ref[...]
    hits = as_bf16(iota((DEVICES, ROWS), 0) == slot >> 3)
    back = jnp.sum(returned_ref[...].T.reshape(GROUP, CAP, DEVICES), axis=0)
    parts = matmul(jnp.concatenate(split3(back), axis=0), hits)
    total = parts[:CAP] + parts[CAP:2 * CAP] + parts[2 * CAP:]
    chosen = jnp.where(iota((CAP, ROWS), 0) == slot & (CAP - 1), total, 0.0)
    scores[...] = jnp.sum(chosen, axis=0, keepdims=True) * scale_ref[...]
    stores.append(pltpu.make_async_copy(scores, scores_hbm, out_sem.at[1]))
    stores[-1].start()
    for store in stores:
        store.wait()


def final(returned, slot, scale, centroids):
    vmem = pl.BlockSpec(memory_space=pltpu.VMEM)
    hbm = pl.BlockSpec(memory_space=pl.ANY)
    return pl.pallas_call(
        final_kernel,
        out_shape=(
            jax.ShapeDtypeStruct((CLUSTER_DEV, WIDTH), jnp.bfloat16),
            jax.ShapeDtypeStruct((1, ROWS), jnp.float32),
        ),
        in_specs=[vmem] * 4,
        out_specs=(hbm, hbm),
        scratch_shapes=[pltpu.VMEM((1, ROWS), jnp.float32), pltpu.SemaphoreType.DMA((2,))],
        compiler_params=pltpu.CompilerParams(vmem_limit_bytes=16 * 1024 * 1024),
    )(returned, slot, scale, centroids)


def body(embeddings, cluster_ids, keep_flags):
    outgoing, slot = pack(cluster_ids.reshape(1, ROWS), keep_flags.reshape(1, ROWS), embeddings)
    arrived = lax.all_to_all(outgoing, AXES, split_axis=0, concat_axis=0, tiled=True)
    centroids, products, row_scale = middle(arrived, embeddings)
    returned = lax.all_to_all(products, AXES, split_axis=0, concat_axis=0, tiled=True)
    centroids, scores = final(returned, slot, row_scale, centroids)
    return (centroids, scores.reshape(ROWS))


def solution(mesh):
    in_specs = (P(AXES, None), P(AXES), P(AXES))
    out_specs = (P(AXES, None), P(AXES))
    return jax.shard_map(body, mesh=mesh, in_specs=in_specs, out_specs=out_specs, check_vma=False)
```
